128 devices in a mesh: row: 8 (over z, y_lo), col: 16 (over y_hi, x, core).
Axes of the slice: x: 4, y: 4 (y_hi: 2, y_lo: 2; y = y_hi * 2 + y_lo), z: 4, core: 2. Of those that a mesh axis runs over, the one named last changes fastest.
Arguments:
- points: float32 [4, 4, 1048576], P(None, None, ('row', 'col')), may hold values from -0.4 to 1.4, as said below
- density: float32 [1048576], P(('row', 'col')), may hold values from -6 to 6
- near_pairs: int32 [768, 2], P(('row', 'col')), may hold values from 0 to 255, as said below
- far_pairs: int32 [2048, 2], P(('row', 'col')), may hold values from 0 to 255, as said below
- near_count: int32 [128], P(('row', 'col')), may hold values from 1 to 6
- far_count: int32 [128], P(('row', 'col')), may hold values from 1 to 16
Outputs:
- potential: float32 [1048576], P(('row', 'col'))
The draws below stay inside these ranges and needn't reach their ends.
Inputs may be any that keep to these rules, and one draw needn't show every extreme that they name: `near_pairs`: the first column indexes target band blocks and the second source band blocks (below 128). On device (r, c) the first column lies in c * 16 to c * 16 + 15, so every near target block is one of the device's own blocks. The first slot of each device names one of its own blocks k as (c * 16 + k, r * 16 + k). `far_pairs`: the first column indexes target band blocks (below 256), the second source band blocks (below 128). `points`: weights (entry 3) lie in 0.01 to 0.04; coordinates in -0.4 to 1.4.
All inputs are finite; a program needn't handle non-finite values.
Results may differ from the reference program's by a relative error of at most 0.0003.
Values sent between devices are 32-bit elements; how exact they have to be, the bound alone decides.
A program may use at most 64 MiB of HBM per device.

```python
import jax
import jax.numpy as jnp
from jax import lax

BLK = 512
QUAD = 4
BPD = 16
NNEAR = 6
NFAR = 16
PANELS = 1048576
N_ROW = 8
N_COL = 16
DEVICES = 128


def draw_points(key, part):
    first, second, third = jax.random.split(key, 3)
    center = jax.random.uniform(first, (3, 1, PANELS), jnp.float32, 0.0, 1.0)
    weight = jnp.exp(jax.random.uniform(third, (1, QUAD, PANELS), jnp.float32, jnp.log(0.01), jnp.log(0.04)))
    offset = jnp.clip(0.08 * jax.random.normal(second, (3, QUAD, PANELS), jnp.float32), -0.4, 0.4)
    return jnp.concatenate([center + offset, weight], axis=0).astype(jnp.float32)


def near_list(key):
    first, second, third = jax.random.split(key, 3)
    dev = jnp.arange(DEVICES, dtype=jnp.int32)
    own = jax.random.randint(first, (DEVICES, NNEAR), 0, BPD)
    col_a = (dev % N_COL)[:, None] * BPD + own
    col_b = jax.random.randint(second, (DEVICES, NNEAR), 0, N_ROW * BPD)
    which = jax.random.randint(third, (DEVICES,), 0, BPD)
    col_a = col_a.at[:, 0].set(dev % N_COL * BPD + which)
    col_b = col_b.at[:, 0].set(dev // N_COL * BPD + which)
    col_a = col_a.at[N_COL - 1, 1].set(N_COL * BPD - 1)
    col_b = col_b.at[N_COL - 1, 1].set(0)
    return jnp.stack([col_a.reshape(-1), col_b.reshape(-1)], axis=1).astype(jnp.int32)


def far_list(key):
    first, second = jax.random.split(key, 2)
    col_a = jax.random.randint(first, (DEVICES, NFAR), 0, N_COL * BPD)
    col_b = jax.random.randint(second, (DEVICES, NFAR), 0, N_ROW * BPD)
    col_a = col_a.at[0, 0].set(N_COL * BPD - 1)
    col_b = col_b.at[0, 0].set(0)
    return jnp.stack([col_a.reshape(-1), col_b.reshape(-1)], axis=1).astype(jnp.int32)


def draw_near_pairs(key, part):
    return near_list(jax.random.fold_in(key, 11))


def draw_far_pairs(key, part):
    return far_list(jax.random.fold_in(key, 12))


def skewed_counts(key, slots):
    first, second, third = jax.random.split(key, 3)
    left = jax.random.randint(first, (DEVICES,), 0, slots)
    right = jax.random.randint(second, (DEVICES,), 0, slots)
    counts = 1 + left * right // (slots - 1)
    busy = jax.random.randint(third, (), 0, DEVICES)
    return counts.at[busy].set(slots).astype(jnp.int32)


def draw_near_count(key, part):
    return skewed_counts(jax.random.fold_in(key, 21), NNEAR)


def draw_far_count(key, part):
    return skewed_counts(jax.random.fold_in(key, 22), NFAR)


def block_levels(key, extent, cuts, low, top_value):
    factor_of = 1.0
    for position, parts in cuts:
        draws = jax.random.uniform(jax.random.fold_in(jax.random.fold_in(key, 6), position), (parts,), jnp.float32, low / len(cuts), top_value / len(cuts))
        factor_of = factor_of * jnp.repeat(jnp.exp(draws), extent[position] // parts).reshape((-1,) + (1,) * (len(extent) - 1 - position))
    return factor_of


def noise(own_key, dims, spread, reach, cuts=(), held_as=jnp.bfloat16):
    values = jax.random.normal(own_key, dims, jnp.float32) * spread
    if len(cuts) > 0:
        values = block_levels(own_key, dims, cuts, -0.22, 0.18) * values
    return jnp.clip(values, min=-reach, max=reach).astype(held_as)


def setup_inputs(seed: int = 0) -> dict:
    key_of = jax.random.split(jax.random.key(seed), 7)
    return {
        "points": draw_points(jax.random.fold_in(key_of[6], 71), 0),
        "density": noise(key_of[1], (PANELS,), 1.0, 6.0, ((0, 128),), jnp.float32),
        "near_pairs": draw_near_pairs(jax.random.fold_in(key_of[6], 71), 0),
        "far_pairs": draw_far_pairs(jax.random.fold_in(key_of[6], 71), 0),
        "near_count": draw_near_count(jax.random.fold_in(key_of[6], 71), 0),
        "far_count": draw_far_count(jax.random.fold_in(key_of[6], 71), 0),
    }


soft_sq = 0.0004

def centroid(block):
    weight = lax.optimization_barrier(jnp.sum(block[3], axis=0))
    place = lax.optimization_barrier(jnp.sum(block[:3] * block[3][None], axis=1)) / weight[None]
    return (place, weight)

def far_tile(left, right):
    place_i, weight_i = centroid(left)
    place_j, weight_j = centroid(right)
    dist = jnp.zeros((left.shape[2], right.shape[2]), jnp.float32)
    for k in range(3):
        diff = place_i[k][:, None] - place_j[k][None, :]
        dist = dist + diff * diff
    return weight_i[:, None] * weight_j[None, :] * lax.rsqrt(dist + soft_sq)

def near_tile(left, right):
    total = jnp.zeros((left.shape[2], right.shape[2]), jnp.float32)
    for u in range(left.shape[1]):
        for v in range(right.shape[1]):
            dist = jnp.zeros((left.shape[2], right.shape[2]), jnp.float32)
            for k in range(3):
                diff = left[k, u][:, None] - right[k, v][None, :]
                dist = dist + diff * diff
            total = total + left[3, u][:, None] * right[3, v][None, :] * lax.rsqrt(dist + soft_sq)
    return total

def run_list(field, blocked, dens, pairs, counts, slots, tile_fn):

    def step(acc, s):
        dev = s // slots
        r = dev // N_COL
        c = dev % N_COL
        a = pairs[s, 0]
        b = pairs[s, 1]
        big_i = ((r * N_COL + a // BPD) * BPD + a % BPD).astype(jnp.int32)
        big_j = ((b // BPD * N_COL + c) * BPD + b % BPD).astype(jnp.int32)
        valid = s % slots < counts[dev]
        mirror = jnp.where(big_i == big_j, 0.0, 1.0).astype(jnp.float32)

        def compute(acc_in):
            left = lax.dynamic_index_in_dim(blocked, big_i, 2, keepdims=False)
            right = lax.dynamic_index_in_dim(blocked, big_j, 2, keepdims=False)
            tile = tile_fn(left, right)
            dens_i = lax.dynamic_index_in_dim(dens, big_i, 0, keepdims=False)
            dens_j = lax.dynamic_index_in_dim(dens, big_j, 0, keepdims=False)
            to_rows = jnp.dot(tile, dens_j, precision=lax.Precision.HIGHEST)
            to_cols = mirror * jnp.dot(dens_i, tile, precision=lax.Precision.HIGHEST)
            acc_in = acc_in.at[big_i].add(to_rows)
            return acc_in.at[big_j].add(to_cols)
        return (lax.cond(valid, compute, lambda x: x, acc), None)
    field, _ = lax.scan(step, field, jnp.arange(pairs.shape[0], dtype=jnp.int32))
    return field

def reference(points, density, near_pairs, far_pairs, near_count, far_count):
    nblk = PANELS // BLK
    blocked = points.reshape(4, points.shape[1], nblk, BLK)
    dens = density.reshape(nblk, BLK)
    field = jnp.zeros((nblk, BLK), jnp.float32)
    field = run_list(field, blocked, dens, near_pairs, near_count, NNEAR, near_tile)
    field = run_list(field, blocked, dens, far_pairs, far_count, NFAR, far_tile)
    return field.reshape(PANELS)
```

```python
import jax
import jax.numpy as jnp
from jax import lax
from jax.experimental import pallas as pl
from jax.experimental.pallas import tpu as pltpu
from jax.sharding import PartitionSpec as P

BLK = 512
BPD = 16
NNEAR = 6
NFAR = 16
N_ROW = 8
N_COL = 16
soft_sq = 0.0004

MESH = pl.DeviceIdType.MESH
F32 = jnp.float32
BF16 = jnp.bfloat16
NREM = NNEAR - 1
LIST = 64


def vmem(*shape, dtype=F32):
    return pltpu.VMEM(shape, dtype)


def owner_of(block):
    return lax.shift_right_logical(block, 4)


def within(block):
    return block & (BPD - 1)


def same_rows(a, b):
    return jnp.full((1, BLK), a, jnp.int32) == jnp.full((1, BLK), b, jnp.int32)


def exchange_kernel(
    pts, dens, npairs, fpairs,
    near_out, near_dens, far_i, far_j, own_dens,
    lists, stage, blocks, cent_i, cent_j, sel_i, sel_j, got_i, got_j, pack, packd, nrecv, nrecvd,
    lsend, lrecv, xsend, xrecv, zsend, zrecv, nsend, nrcv, dsend, drcv, ysend, yrecv,
):
    r = lax.axis_index("row")
    c = lax.axis_index("col")
    z, ylo = r // 2, lax.rem(r, 2)
    yhi, xc = c // 8, lax.rem(c, 8)
    x, core = xc // 2, lax.rem(xc, 2)
    row_peers = [(lax.rem(r + i, N_ROW), c) for i in range(1, N_ROW)]
    x_peers = [(r, yhi * 8 + lax.rem(x + i, 4) * 2 + core) for i in range(1, 4)]
    core_peer = (r, yhi * 8 + x * 2 + 1 - core)
    y_far = (r, lax.rem(c + 8, N_COL))
    y_near = (r + 1 - 2 * ylo, c)

    barrier = pltpu.get_barrier_semaphore()
    everyone = row_peers + x_peers + [core_peer, y_far]
    for p in everyone:
        pl.semaphore_signal(barrier, inc=1, device_id=p, device_id_type=MESH)

    for s in range(NNEAR):
        stage[s] = npairs[s, 0]
        stage[NNEAR + s] = npairs[s, 1]
    for s in range(NFAR):
        stage[16 + s] = fpairs[s, 0]
        stage[32 + s] = fpairs[s, 1]

    def centroid(k, _):
        cols = pl.ds(pl.multiple_of(k * BLK, BLK), BLK)
        blocks[k] = pts[:, :, cols]
        w = pts[3, :, cols]
        total = jnp.sum(w, axis=0, keepdims=True)
        for d in range(3):
            cent_i[xc, d, pl.ds(k, 1), :] = jnp.sum(pts[d, :, cols] * w, axis=0, keepdims=True) / total
        cent_i[xc, 3, pl.ds(k, 1), :] = total
        return 0

    lax.fori_loop(0, BPD, centroid, 0)
    for q in range(4):
        cent_i[xc, 4, :, q * 128 : (q + 1) * 128] = dens[pl.ds(q, BPD, stride=4), :]
    cent_j[z] = cent_i[xc]
    own_dens[...] = cent_i[xc, 4]

    pl.semaphore_wait(barrier, len(everyone))

    def remote(src, dst, send, recv, peer):
        copy = pltpu.make_async_remote_copy(
            src_ref=src, dst_ref=dst, send_sem=send, recv_sem=recv, device_id=peer, device_id_type=MESH
        )
        copy.start()
        return copy

    pending = []
    list_copies = [remote(stage, lists.at[r], lsend.at[i], lrecv.at[i], p) for i, p in enumerate(row_peers)]
    list_copies.append(remote(stage, lists.at[N_ROW], lsend.at[7], lrecv.at[7], y_far))
    x_copies = [remote(cent_i.at[xc], cent_i.at[xc], xsend.at[i], xrecv.at[i], p) for i, p in enumerate(x_peers)]
    x_copies.append(remote(cent_i.at[xc], cent_i.at[xc], xsend.at[3], xrecv.at[3], core_peer))
    z_copies = [
        remote(cent_j.at[z], cent_j.at[z], zsend.at[i - 1], zrecv.at[i - 1], (lax.rem(z + i, 4) * 2 + ylo, c))
        for i in range(1, 4)
    ]

    for copy in list_copies:
        copy.wait_recv()
    near_copies = []
    for i in range(N_ROW):
        peer = lax.rem(r + i, N_ROW)
        if i == 0:
            source = stage
        else:
            source = lists.at[peer]

        def fill(s, _, i=i, source=source):
            k = within(source[NNEAR + 1 + s])
            if i == 0:
                nrecv[r, s] = blocks[k]
                nrecvd[r, pl.ds(s, 1), :] = own_dens[pl.ds(k, 1), :]
            else:
                pack[i - 1, s] = blocks[k]
                packd[i - 1, pl.ds(s, 1), :] = own_dens[pl.ds(k, 1), :]
            return 0

        lax.fori_loop(0, NREM, fill, 0)
        if i > 0:
            near_copies.append(remote(pack.at[i - 1], nrecv.at[r], nsend.at[i - 1], nrcv.at[i - 1], (peer, c)))
            near_copies.append(remote(packd.at[i - 1], nrecvd.at[r], dsend.at[i - 1], drcv.at[i - 1], (peer, c)))

    relays = []
    for i in range(1, 4):
        x_copies[i - 1].wait_recv()
        g = lax.rem(x - i + 4, 4) * 2 + core
        relays.append(remote(cent_i.at[g], cent_i.at[g], xsend.at[3 + i], xrecv.at[3 + i], core_peer))
    x_copies[3].wait_recv()
    for copy in relays:
        copy.wait_recv()

    def choose_i(s, _):
        a = lists[N_ROW, 16 + s]
        g, k = owner_of(a) & 7, within(a)
        for f in range(5):
            sel_i[f, pl.ds(s, 1), :] = cent_i[g, f, pl.ds(k, 1), :]
        return 0

    lax.fori_loop(0, NFAR, choose_i, 0)
    y_copies = [remote(sel_i, got_i, ysend.at[0], yrecv.at[0], y_far)]

    for copy in z_copies:
        copy.wait_recv()
    near_row = y_near[0]

    def choose_j(s, _):
        b = lists[near_row, 32 + s]
        g, k = lax.shift_right_logical(owner_of(b), 1), within(b)
        for f in range(5):
            sel_j[f, pl.ds(s, 1), :] = cent_j[g, f, pl.ds(k, 1), :]
        return 0

    lax.fori_loop(0, NFAR, choose_j, 0)
    y_copies.append(remote(sel_j, got_j, ysend.at[1], yrecv.at[1], y_near))

    y_copies[0].wait_recv()

    def take_i(s, _):
        a = stage[16 + s]
        owner, k = owner_of(a), within(a)
        here = same_rows(lax.shift_right_logical(owner, 3), yhi)
        for f in range(5):
            far_i[f, pl.ds(s, 1), :] = jnp.where(
                here, cent_i[owner & 7, f, pl.ds(k, 1), :], got_i[f, pl.ds(s, 1), :]
            )
        return 0

    lax.fori_loop(0, NFAR, take_i, 0)
    y_copies[1].wait_recv()

    def take_j(s, _):
        b = stage[32 + s]
        owner, k = owner_of(b), within(b)
        here = same_rows(owner & 1, ylo)
        for f in range(5):
            far_j[f, pl.ds(s, 1), :] = jnp.where(
                here, cent_j[lax.shift_right_logical(owner, 1), f, pl.ds(k, 1), :], got_j[f, pl.ds(s, 1), :]
            )
        return 0

    lax.fori_loop(0, NFAR, take_j, 0)

    for copy in near_copies:
        copy.wait_recv()

    def take_near(s, _):
        owner = owner_of(stage[NNEAR + 1 + s])
        near_out[s] = nrecv[owner, s]
        near_dens[pl.ds(s, 1), :] = nrecvd[owner, pl.ds(s, 1), :]
        return 0

    lax.fori_loop(0, NREM, take_near, 0)
    near_dens[NREM:, :] = jnp.zeros((8 - NREM, BLK), F32)
    for copy in list_copies + x_copies + relays + z_copies + near_copies + y_copies:
        copy.wait_send()


def exchange(pts, dens, npairs, fpairs):
    dma = pltpu.SemaphoreType.DMA
    shape = jax.ShapeDtypeStruct
    return pl.pallas_call(
        exchange_kernel,
        out_shape=(
            shape((NREM, 4, 4, BLK), F32),
            shape((8, BLK), F32),
            shape((5, NFAR, BLK), F32),
            shape((5, NFAR, BLK), F32),
            shape((BPD, BLK), F32),
        ),
        in_specs=[pl.BlockSpec(memory_space=pltpu.VMEM)] * 2 + [pl.BlockSpec(memory_space=pltpu.SMEM)] * 2,
        out_specs=[pl.BlockSpec(memory_space=pltpu.VMEM)] * 5,
        scratch_shapes=[
            pltpu.SMEM((N_ROW + 1, LIST), jnp.int32),
            pltpu.SMEM((LIST,), jnp.int32),
            vmem(BPD, 4, 4, BLK),
            vmem(8, 5, BPD, BLK),
            vmem(4, 5, BPD, BLK),
            vmem(5, NFAR, BLK),
            vmem(5, NFAR, BLK),
            vmem(5, NFAR, BLK),
            vmem(5, NFAR, BLK),
            vmem(N_ROW - 1, NREM, 4, 4, BLK),
            vmem(N_ROW - 1, 8, BLK),
            vmem(N_ROW, NREM, 4, 4, BLK),
            vmem(N_ROW, 8, BLK),
            dma((8,)), dma((8,)), dma((7,)), dma((7,)), dma((3,)), dma((3,)),
            dma((7,)), dma((7,)), dma((7,)), dma((7,)), dma((2,)), dma((2,)),
        ],
        compiler_params=pltpu.CompilerParams(collective_id=0, has_side_effects=True, vmem_limit_bytes=40 << 20),
    )(pts, dens, npairs, fpairs)


def split3(v):
    hi = v.astype(BF16).astype(F32)
    rest = v - hi
    mid = rest.astype(BF16).astype(F32)
    return hi, mid, rest - mid


def left_rows(px, py, pz, w):
    inv = 1.0 / (w * w)
    rows = []
    for v in ((px * px + py * py + pz * pz + soft_sq) * inv, inv, -2.0 * px * inv, -2.0 * py * inv, -2.0 * pz * inv):
        hi, mid, lo = split3(v)
        rows += [hi, hi, mid, mid, hi, lo]
    return rows


def right_rows(px, py, pz, w):
    inv = 1.0 / (w * w)
    rows = []
    for v in (inv, (px * px + py * py + pz * pz) * inv, px * inv, py * inv, pz * inv):
        hi, mid, lo = split3(v)
        rows += [hi, mid, hi, mid, lo, hi]
    return rows


def put_rows(ref, rows):
    n = rows[0].shape[0]
    for k, v in enumerate(rows):
        ref[k * n : (k + 1) * n, :] = v


def tile_kernel(
    pts, own_dens, near_pts, near_dens, far_i, far_j, npairs, fpairs, ncount, fcount,
    own_out, row_msg, col_msg,
    abuf, bbuf, lhs, rhs, tile, pj, dj, cfi, cfj, fa, fb,
):
    r = lax.axis_index("row")
    c = lax.axis_index("col")
    own_out[...] = jnp.zeros((BPD, BLK), F32)
    row_msg[...] = jnp.zeros_like(row_msg)
    col_msg[...] = jnp.zeros_like(col_msg)
    abuf[120:, :] = jnp.zeros((8, BLK), F32)
    bbuf[120:, :] = jnp.zeros((8, BLK), F32)
    fa[30:, :] = jnp.zeros((2, BLK), F32)
    fb[30:, :] = jnp.zeros((2, BLK), F32)
    lane = lax.broadcasted_iota(jnp.int32, (BLK, 128), 1) % 4
    ri = lax.broadcasted_iota(jnp.int32, (128, 128), 0)
    ci = lax.broadcasted_iota(jnp.int32, (128, 128), 1)

    def apply(di, dj):
        turned = jnp.transpose(jnp.broadcast_to(di, (128, BLK)))
        part = None
        to_cols = []
        for q in range(4):
            cols = slice(q * 128, (q + 1) * 128)
            blk = tile[:, cols]
            e = blk * dj[:, cols]
            part = e if part is None else part + e
            to_cols.append(jnp.sum(blk * turned, axis=0, keepdims=True))
        to_rows = jnp.sum(jnp.transpose(part), axis=0, keepdims=True)
        return to_rows, jnp.concatenate(to_cols, axis=1)

    def mirrored(a, b):
        same = (b // BPD == r) & (a // BPD == c) & (lax.rem(a, BPD) == lax.rem(b, BPD))
        return jnp.where(same, 0.0, 1.0).astype(F32)

    def near(s, _):
        a, b = npairs[s, 0], npairs[s, 1]
        k = a - c * BPD
        cols = pl.ds(pl.multiple_of(k * BLK, BLK), BLK)

        @pl.when(s == 0)
        def _():
            pj[...] = pts[:, :, cols]
            dj[...] = own_dens[pl.ds(k, 1), :]

        @pl.when(s > 0)
        def _():
            pj[...] = near_pts[s - 1]
            dj[...] = near_dens[pl.ds(s - 1, 1), :]

        left = [pts[d, :, cols] for d in range(4)]
        mid = [jnp.mean(left[d]) for d in range(3)]
        put_rows(abuf, left_rows(*(left[d] - mid[d] for d in range(3)), left[3]))
        put_rows(bbuf, right_rows(*(pj[d] - mid[d] for d in range(3)), pj[3]))
        at = jnp.transpose(abuf[...]).astype(BF16)
        for u in range(4):
            lhs[u] = jnp.where(lane == u, at, jnp.zeros_like(at))
        bt = bbuf[...].astype(BF16)
        rhs[0] = bt
        for t in range(1, 4):
            shift = jnp.where((ri // 4 == ci // 4) & ((ri % 4 + t) % 4 == ci % 4), 1.0, 0.0).astype(BF16)
            rhs[t] = jnp.dot(shift, bt, preferred_element_type=F32).astype(BF16)
        for t in range(4):
            for h in range(2):
                half = slice(h * 256, (h + 1) * 256)
                acc = None
                for u in range(4):
                    v = lax.rsqrt(jnp.dot(lhs[u], rhs[t][:, half], preferred_element_type=F32))
                    acc = v if acc is None else acc + v
                if t == 0:
                    tile[:, half] = acc
                else:
                    tile[:, half] += acc
        to_rows, to_cols = apply(own_dens[pl.ds(k, 1), :], dj[...])
        own_out[pl.ds(k, 1), :] += to_rows
        col_msg[pl.ds(16 + s, 1), :] = mirrored(a, b) * to_cols
        return 0

    lax.fori_loop(0, ncount[0], near, 0)

    for d in range(3):
        mid = jnp.mean(far_i[d], axis=1, keepdims=True)
        cfi[d] = far_i[d] - mid
        cfj[d] = far_j[d] - mid

    def far(s, _):
        a, b = fpairs[s, 0], fpairs[s, 1]
        one = pl.ds(s, 1)
        put_rows(fa, left_rows(*(cfi[d, one, :] for d in range(3)), far_i[3, one, :]))
        put_rows(fb, right_rows(*(cfj[d, one, :] for d in range(3)), far_j[3, one, :]))
        at = jnp.transpose(fa[...]).astype(BF16)
        bt = fb[...].astype(BF16)
        for h in range(2):
            half = slice(h * 256, (h + 1) * 256)
            tile[:, half] = lax.rsqrt(jnp.dot(at, bt[:, half], preferred_element_type=F32))
        to_rows, to_cols = apply(far_i[4, one, :], far_j[4, one, :])
        row_msg[one, :] = to_rows
        col_msg[one, :] = mirrored(a, b) * to_cols
        return 0

    lax.fori_loop(0, fcount[0], far, 0)

    at_lane = lax.broadcasted_iota(jnp.int32, (1, BLK), 1)
    ids_a = jnp.full((1, BLK), -1, jnp.int32)
    ids_b = jnp.full((1, BLK), -1, jnp.int32)
    for s in range(NFAR):
        ids_a = jnp.where(at_lane == s, fpairs[s, 0], ids_a)
        ids_b = jnp.where(at_lane == s, fpairs[s, 1], ids_b)
    for s in range(NNEAR):
        ids_b = jnp.where(at_lane == 16 + s, npairs[s, 1], ids_b)
    row_msg[16:17, :] = ids_a.astype(F32)
    col_msg[22:23, :] = ids_b.astype(F32)


def tiles(pts, own_dens, near_pts, near_dens, far_i, far_j, npairs, fpairs, ncount, fcount):
    shape = jax.ShapeDtypeStruct
    return pl.pallas_call(
        tile_kernel,
        out_shape=(shape((BPD, BLK), F32), shape((24, BLK), F32), shape((24, BLK), F32)),
        in_specs=[pl.BlockSpec(memory_space=pltpu.VMEM)] * 6 + [pl.BlockSpec(memory_space=pltpu.SMEM)] * 4,
        out_specs=[pl.BlockSpec(memory_space=pltpu.VMEM)] * 3,
        scratch_shapes=[
            vmem(128, BLK),
            vmem(128, BLK),
            vmem(4, BLK, 128, dtype=BF16),
            vmem(4, 128, BLK, dtype=BF16),
            vmem(BLK, BLK),
            vmem(4, 4, BLK),
            vmem(1, BLK),
            vmem(3, NFAR, BLK),
            vmem(3, NFAR, BLK),
            vmem(32, BLK),
            vmem(32, BLK),
        ],
        compiler_params=pltpu.CompilerParams(vmem_limit_bytes=40 << 20),
    )(pts, own_dens, near_pts, near_dens, far_i, far_j, npairs, fpairs, ncount, fcount)


def scatter(ids, base, count, vals):
    place = lax.broadcasted_iota(jnp.int32, (count, 24), 0) + base
    hot = jnp.where(place == ids, 1.0, 0.0).astype(BF16)
    out = None
    for part in split3(vals):
        v = jnp.dot(hot, part.astype(BF16), preferred_element_type=F32)
        out = v if out is None else out + v
    return out


def collect_kernel(
    own, row_msg, col_msg, out,
    row_got, col_got, half, parts, ysend, yrecv, csend, crecv, psend, precv,
):
    r = lax.axis_index("row")
    c = lax.axis_index("col")
    yhi, xc = c // 8, lax.rem(c, 8)
    y_far = (r, lax.rem(c + 8, N_COL))
    row_peers = [(lax.rem(r + i, N_ROW), c) for i in range(1, N_ROW)]
    x_peers = [(r, yhi * 8 + lax.rem(xc + i, 8)) for i in range(1, 8)]
    barrier = pltpu.get_barrier_semaphore()
    everyone = row_peers + x_peers + [y_far]
    for p in everyone:
        pl.semaphore_signal(barrier, inc=1, device_id=p, device_id_type=MESH)
    pl.semaphore_wait(barrier, len(everyone))

    def remote(src, dst, send, recv, peer):
        copy = pltpu.make_async_remote_copy(
            src_ref=src, dst_ref=dst, send_sem=send, recv_sem=recv, device_id=peer, device_id_type=MESH
        )
        copy.start()
        return copy

    y_copy = remote(row_msg, row_got, ysend.at[0], yrecv.at[0], y_far)
    c_copies = [remote(col_msg, col_got.at[i], csend.at[i], crecv.at[i], p) for i, p in enumerate(row_peers)]

    def rows_of(msg):
        return scatter(msg[16:17, 0:24].astype(jnp.int32), yhi * 128, 128, msg[...])

    mine = rows_of(row_msg)
    y_copy.wait_recv()
    total = mine + rows_of(row_got)
    for g in range(8):
        half[g] = total[g * BPD : (g + 1) * BPD, :]
    p_copies = []
    for i, p in enumerate(x_peers):
        to = lax.rem(xc + 1 + i, 8)
        p_copies.append(remote(half.at[to], parts.at[i], psend.at[i], precv.at[i], p))
    acc = own[...] + half[xc]

    def cols_of(msg):
        return scatter(msg[22:23, 0:24].astype(jnp.int32), r * BPD, BPD, msg[...])

    acc = acc + cols_of(col_msg)
    for i, copy in enumerate(c_copies):
        copy.wait_recv()
        acc = acc + cols_of(col_got.at[i])
    for i, copy in enumerate(p_copies):
        copy.wait_recv()
        acc = acc + parts[i]
    for q in range(4):
        out[pl.ds(q, BPD, stride=4), :] = acc[:, q * 128 : (q + 1) * 128]
    for copy in [y_copy] + c_copies + p_copies:
        copy.wait_send()


def collect(own, row_msg, col_msg):
    dma = pltpu.SemaphoreType.DMA
    return pl.pallas_call(
        collect_kernel,
        out_shape=jax.ShapeDtypeStruct((BPD * 4, 128), F32),
        in_specs=[pl.BlockSpec(memory_space=pltpu.VMEM)] * 3,
        out_specs=pl.BlockSpec(memory_space=pltpu.VMEM),
        scratch_shapes=[
            vmem(24, BLK),
            vmem(N_ROW - 1, 24, BLK),
            vmem(8, BPD, BLK),
            vmem(7, BPD, BLK),
            dma((1,)), dma((1,)), dma((7,)), dma((7,)), dma((7,)), dma((7,)),
        ],
        compiler_params=pltpu.CompilerParams(collective_id=1, has_side_effects=True, vmem_limit_bytes=16 << 20),
    )(own, row_msg, col_msg)


def body(points, density, near_pairs, far_pairs, near_count, far_count):
    near_pts, near_dens, far_i, far_j, own_dens = exchange(points, density.reshape(-1, 128), near_pairs, far_pairs)
    own, row_msg, col_msg = tiles(
        points, own_dens, near_pts, near_dens, far_i, far_j, near_pairs, far_pairs, near_count, far_count
    )
    return collect(own, row_msg, col_msg).reshape(-1)


def solution(mesh):
    in_specs = (
        P(None, None, ("row", "col")),
        P(("row", "col")),
        P(("row", "col"), None),
        P(("row", "col"), None),
        P(("row", "col")),
        P(("row", "col")),
    )
    out_specs = P(("row", "col"))
    return jax.shard_map(body, mesh=mesh, in_specs=in_specs, out_specs=out_specs, check_vma=False)
```

```python
import jax
import jax.numpy as jnp
from jax import lax
from jax.experimental import pallas as pl
from jax.experimental.pallas import tpu as pltpu
from jax.sharding import PartitionSpec as P

BLK = 512
BPD = 16
NNEAR = 6
NFAR = 16
N_ROW = 8
N_COL = 16
soft_sq = 0.0004

MESH = pl.DeviceIdType.MESH
F32 = jnp.float32
BF16 = jnp.bfloat16
NREM = NNEAR - 1
LIST = 64


def vmem(*shape, dtype=F32):
    return pltpu.VMEM(shape, dtype)


def owner_of(block):
    return lax.shift_right_logical(block, 4)


def within(block):
    return block & (BPD - 1)


def row_mask(a, b, op):
    return op(jnp.full((1, BLK), a, jnp.int32), jnp.full((1, BLK), b, jnp.int32))


def same_rows(a, b):
    return row_mask(a, b, lambda x, y: x == y)


def split3(v):
    hi = v.astype(BF16).astype(F32)
    rest = v - hi
    mid = rest.astype(BF16).astype(F32)
    return hi, mid, rest - mid


def left_rows(px, py, pz, w):
    inv = 1.0 / (w * w)
    rows = []
    for v in ((px * px + py * py + pz * pz + soft_sq) * inv, inv, -2.0 * px * inv, -2.0 * py * inv, -2.0 * pz * inv):
        hi, mid, lo = split3(v)
        rows += [hi, hi, mid, mid, hi, lo]
    return rows


def right_rows(px, py, pz, w):
    inv = 1.0 / (w * w)
    rows = []
    for v in (inv, (px * px + py * py + pz * pz) * inv, px * inv, py * inv, pz * inv):
        hi, mid, lo = split3(v)
        rows += [hi, mid, hi, mid, lo, hi]
    return rows


def put_rows(ref, rows):
    n = rows[0].shape[0]
    for k, v in enumerate(rows):
        ref[k * n : (k + 1) * n, :] = v


def scatter(ids, base, count, vals):
    place = lax.broadcasted_iota(jnp.int32, (count, vals.shape[0]), 0) + base
    hot = jnp.where(place == ids, 1.0, 0.0).astype(BF16)
    out = None
    for part in split3(vals):
        v = jnp.dot(hot, part.astype(BF16), preferred_element_type=F32)
        out = v if out is None else out + v
    return out


def gathered(msgs, base, count, at):
    m, n, _ = msgs.shape
    ids = jnp.concatenate([msgs[i, at : at + 1, 0:n] for i in range(m)], axis=1).astype(jnp.int32)
    return scatter(ids, base, count, msgs[...].reshape(m * n, BLK))


def potential_kernel(
    pts_hbm, dens_hbm, npairs, fpairs, ncount, fcount,
    out,
    lists, stage, blocks, dens, cent_i, cent_j, own_dens, sel_i, sel_j, got_i, got_j, far_i, far_j,
    pack, packd, nrecv, nrecvd,
    abuf, bbuf, left, turned, mids, lhs, rhs, tile, pj, fa, fb,
    rows_all, cols_all, near_all, half, parts,
    load, lsend, lrecv, xsend, xrecv, zsend, zrecv, nsend, nrcv, dsend, drcv, ysend, yrecv,
    msend, mrecv, fsend, frecv, csend, crecv, psend, precv,
):
    r = lax.axis_index("row")
    c = lax.axis_index("col")
    z, ylo = r // 2, lax.rem(r, 2)
    yhi, xc = c // 8, lax.rem(c, 8)
    x, core = xc // 2, lax.rem(xc, 2)
    row_peers = [(lax.rem(r + i, N_ROW), c) for i in range(1, N_ROW)]
    xc_peers = [(r, yhi * 8 + lax.rem(xc + i, 8)) for i in range(1, 8)]
    x_peers = [(r, yhi * 8 + lax.rem(x + i, 4) * 2 + core) for i in range(1, 4)]
    core_peer = (r, yhi * 8 + x * 2 + 1 - core)
    y_far = (r, lax.rem(c + 8, N_COL))
    y_near = (r + 1 - 2 * ylo, c)

    barrier = pltpu.get_barrier_semaphore()
    everyone = row_peers + xc_peers + [y_far]
    for p in everyone:
        pl.semaphore_signal(barrier, inc=1, device_id=p, device_id_type=MESH)

    loads = [
        pltpu.make_async_copy(pts_hbm.at[:, :, pl.ds(k * BLK, BLK)], blocks.at[k], load.at[k]) for k in range(BPD)
    ]
    loads.append(pltpu.make_async_copy(dens_hbm, dens, load.at[BPD]))
    for copy in loads:
        copy.start()

    for s in range(NNEAR):
        stage[s] = npairs[0, s]
        stage[NNEAR + s] = npairs[1, s]
    for s in range(NFAR):
        stage[16 + s] = fpairs[0, s]
        stage[32 + s] = fpairs[1, s]
    abuf[120:, :] = jnp.zeros((8, BLK), F32)
    bbuf[120:, :] = jnp.zeros((8, BLK), F32)
    fa[30:, :] = jnp.zeros((2, BLK), F32)
    fb[30:, :] = jnp.zeros((2, BLK), F32)
    for copy in loads:
        copy.wait()

    def centroid(k, _):
        p = blocks[k]
        w = p[3]
        total = jnp.sum(w, axis=0, keepdims=True)
        for d in range(3):
            cent_i[xc, d, pl.ds(k, 1), :] = jnp.sum(p[d] * w, axis=0, keepdims=True) / total
        cent_i[xc, 3, pl.ds(k, 1), :] = total
        return 0

    lax.fori_loop(0, BPD, centroid, 0)
    for q in range(4):
        own_dens[:, q * 128 : (q + 1) * 128] = dens[pl.ds(q, BPD, stride=4), :]
    cent_i[xc, 4] = own_dens[...]
    cent_j[z] = cent_i[xc]

    pl.semaphore_wait(barrier, len(everyone))

    def remote(src, dst, send, recv, peer):
        return pltpu.make_async_remote_copy(
            src_ref=src, dst_ref=dst, send_sem=send, recv_sem=recv, device_id=peer, device_id_type=MESH
        )

    started = []

    def go(copy):
        copy.start()
        started.append(copy)
        return copy

    list_copies = [go(remote(stage, lists.at[r], lsend.at[i], lrecv.at[i], p)) for i, p in enumerate(row_peers)]
    list_copies.append(go(remote(stage, lists.at[N_ROW], lsend.at[7], lrecv.at[7], y_far)))
    x_copies = [go(remote(cent_i.at[xc], cent_i.at[xc], xsend.at[i], xrecv.at[i], p)) for i, p in enumerate(x_peers)]
    x_copies.append(go(remote(cent_i.at[xc], cent_i.at[xc], xsend.at[3], xrecv.at[3], core_peer)))
    z_copies = [
        go(remote(cent_j.at[z], cent_j.at[z], zsend.at[i - 1], zrecv.at[i - 1], (lax.rem(z + i, 4) * 2 + ylo, c)))
        for i in range(1, 4)
    ]

    lane = lax.broadcasted_iota(jnp.int32, (BLK, 128), 1) % 4
    ri = lax.broadcasted_iota(jnp.int32, (128, 128), 0)
    ci = lax.broadcasted_iota(jnp.int32, (128, 128), 1)

    def turn(di):
        return jnp.transpose(jnp.broadcast_to(di, (128, BLK)))

    def apply(column, dj):
        part = None
        to_cols = []
        for q in range(4):
            cols = slice(q * 128, (q + 1) * 128)
            blk = tile[:, cols]
            e = blk * dj[:, cols]
            part = e if part is None else part + e
            to_cols.append(jnp.sum(blk * column, axis=0, keepdims=True))
        to_rows = jnp.sum(jnp.transpose(part), axis=0, keepdims=True)
        return to_rows, jnp.concatenate(to_cols, axis=1)

    def masks(a, b, s, count):
        used = row_mask(s, count, lambda m, n: m < n)
        other = row_mask((b ^ (r * BPD + within(a))) | (owner_of(a) ^ c), 0, lambda m, n: m != n)
        return used, used & other

    def near_left(s, _):
        k = within(stage[s])
        p = blocks[k]
        mid = [jnp.mean(p[d]) for d in range(3)]
        put_rows(abuf, left_rows(*(p[d] - mid[d] for d in range(3)), p[3]))
        left[s] = jnp.transpose(abuf[...]).astype(BF16)
        turned[s] = turn(own_dens[pl.ds(k, 1), :])
        for d in range(3):
            mids[s, d : d + 1, :] = jnp.full((1, BLK), mid[d], F32)
        return 0

    def near_right(s, p, dj):
        put_rows(bbuf, right_rows(*(p[d] - mids[s, d : d + 1, :] for d in range(3)), p[3]))
        bt = bbuf[...].astype(BF16)
        rhs[0] = bt
        for t in range(1, 4):
            shift = jnp.where((ri // 4 == ci // 4) & ((ri % 4 + t) % 4 == ci % 4), 1.0, 0.0).astype(BF16)
            rhs[t] = jnp.dot(shift, bt, preferred_element_type=F32).astype(BF16)
        at = left[s]
        for u in range(4):
            lhs[u] = jnp.where(lane == u, at, jnp.zeros_like(at))
        for t in range(4):
            for h in range(2):
                span = slice(h * 256, (h + 1) * 256)
                acc = None
                for u in range(4):
                    v = lax.rsqrt(jnp.dot(lhs[u], rhs[t][:, span], preferred_element_type=F32))
                    acc = v if acc is None else acc + v
                if t == 0:
                    tile[:, span] = acc
                else:
                    tile[:, span] += acc
        to_rows, to_cols = apply(turned[s], dj)
        used, mirror = masks(stage[s], stage[NNEAR + s], s, ncount[0])
        near_all[8, pl.ds(s, 1), :] = jnp.where(used, to_rows, 0.0)
        near_all[7, pl.ds(s, 1), :] = jnp.where(mirror, to_cols, 0.0)

    def near_copy(i, s):
        peer = lax.rem(r + i, N_ROW)
        return remote(pack.at[i - 1, s], nrecv.at[s, r], nsend.at[i - 1, s], nrcv.at[i - 1, s], (peer, c))

    def near_slot(s):
        for i in range(1, N_ROW):
            near_copy(i, s).wait_recv()
        b = stage[NNEAR + 1 + s]
        owner = owner_of(b)
        p = nrecv[s, 0]
        d = nrecvd[0, pl.ds(s, 1), :]
        for o in range(1, N_ROW):
            hit = jnp.full((4, 4, BLK), owner, jnp.int32) == o
            p = jnp.where(hit, nrecv[s, o], p)
            d = jnp.where(same_rows(owner, o), nrecvd[o, pl.ds(s, 1), :], d)
        pj[...] = p
        near_right(s + 1, pj, d)

    for m in range(7, 9):
        near_all[m] = jnp.zeros((8, BLK), F32)
    lax.fori_loop(0, NNEAR, near_left, 0)

    for copy in list_copies:
        copy.wait_recv()
    dens_copies = []
    for i in range(N_ROW):
        peer = lax.rem(r + i, N_ROW)
        source = stage if i == 0 else lists.at[peer]
        for s in range(NREM):
            row = own_dens[pl.ds(within(source[NNEAR + 1 + s]), 1), :]
            if i == 0:
                nrecvd[r, s : s + 1, :] = row
            else:
                packd[i - 1, s : s + 1, :] = row
        if i > 0:
            packd[i - 1, NREM:, :] = jnp.zeros((8 - NREM, BLK), F32)
            dens_copies.append(go(remote(packd.at[i - 1], nrecvd.at[r], dsend.at[i - 1], drcv.at[i - 1], (peer, c))))

    def fill(s, _):
        nrecv[s, r] = blocks[within(stage[NNEAR + 1 + s])]
        for i in range(1, N_ROW):
            pack[i - 1, s] = blocks[within(lists[lax.rem(r + i, N_ROW), NNEAR + 1 + s])]
            near_copy(i, s).start()
        return 0

    lax.fori_loop(0, NREM, fill, 0)

    k0 = within(stage[0])
    pj[...] = blocks[k0]
    near_right(0, pj, own_dens[pl.ds(k0, 1), :])

    relays = []
    for i in range(1, 4):
        x_copies[i - 1].wait_recv()
        g = lax.rem(x - i + 4, 4) * 2 + core
        relays.append(go(remote(cent_i.at[g], cent_i.at[g], xsend.at[3 + i], xrecv.at[3 + i], core_peer)))
    for copy in z_copies:
        copy.wait_recv()
    near_row = y_near[0]

    def choose_j(s, _):
        b = lists[near_row, 32 + s]
        g, k = lax.shift_right_logical(owner_of(b), 1), within(b)
        for f in range(5):
            sel_j[f, pl.ds(s, 1), :] = cent_j[g, f, pl.ds(k, 1), :]
        return 0

    lax.fori_loop(0, NFAR, choose_j, 0)
    yj_copy = go(remote(sel_j, got_j, ysend.at[1], yrecv.at[1], y_near))
    x_copies[3].wait_recv()
    for copy in relays:
        copy.wait_recv()

    def choose_i(s, _):
        a = lists[N_ROW, 16 + s]
        g, k = owner_of(a) & 7, within(a)
        for f in range(5):
            sel_i[f, pl.ds(s, 1), :] = cent_i[g, f, pl.ds(k, 1), :]
        return 0

    lax.fori_loop(0, NFAR, choose_i, 0)
    yi_copy = go(remote(sel_i, got_i, ysend.at[0], yrecv.at[0], y_far))

    for copy in dens_copies:
        copy.wait_recv()
    near_slot(0)

    yj_copy.wait_recv()
    yi_copy.wait_recv()

    def take(s, _):
        a, b = stage[16 + s], stage[32 + s]
        owner, k = owner_of(a), within(a)
        here = same_rows(lax.shift_right_logical(owner, 3), yhi)
        one = pl.ds(s, 1)
        for f in range(5):
            far_i[f, one, :] = jnp.where(here, cent_i[owner & 7, f, pl.ds(k, 1), :], got_i[f, one, :])
        owner, k = owner_of(b), within(b)
        here = same_rows(owner & 1, ylo)
        for f in range(5):
            far_j[f, one, :] = jnp.where(
                here, cent_j[lax.shift_right_logical(owner, 1), f, pl.ds(k, 1), :], got_j[f, one, :]
            )
        return 0

    lax.fori_loop(0, NFAR, take, 0)
    for d in range(3):
        mid = jnp.mean(far_i[d], axis=1, keepdims=True)
        far_i[d] = far_i[d] - mid
        far_j[d] = far_j[d] - mid

    at_lane = lax.broadcasted_iota(jnp.int32, (1, BLK), 1)

    def ids_of(values, n):
        ids = jnp.full((1, BLK), -1, jnp.int32)
        for s in range(n):
            ids = jnp.where(at_lane == s, values(s), ids)
        return ids.astype(F32)

    for ref, first in ((rows_all.at[0], 16), (cols_all.at[7], 32)):
        ref[16:, :] = jnp.zeros((8, BLK), F32)
        ref[16:17, :] = ids_of(lambda s, first=first: stage[first + s], NFAR)

    def far(s, _):
        one = pl.ds(s, 1)
        put_rows(fa, left_rows(*(far_i[d, one, :] for d in range(4))))
        put_rows(fb, right_rows(*(far_j[d, one, :] for d in range(4))))
        at = jnp.transpose(fa[...]).astype(BF16)
        bt = fb[...].astype(BF16)
        for h in range(2):
            span = slice(h * 256, (h + 1) * 256)
            tile[:, span] = lax.rsqrt(jnp.dot(at, bt[:, span], preferred_element_type=F32))
        to_rows, to_cols = apply(turn(far_i[4, one, :]), far_j[4, one, :])
        used, mirror = masks(stage[16 + s], stage[32 + s], s, fcount[0])
        rows_all[0, one, :] = jnp.where(used, to_rows, 0.0)
        cols_all[7, one, :] = jnp.where(mirror, to_cols, 0.0)
        return 0

    lax.fori_loop(0, NFAR, far, 0)
    m_copy = go(remote(rows_all.at[0], rows_all.at[1], msend.at[0], mrecv.at[0], y_far))
    f_copies = [
        go(remote(cols_all.at[7], cols_all.at[i], fsend.at[i], frecv.at[i], p)) for i, p in enumerate(row_peers)
    ]

    near_slot(1)

    m_copy.wait_recv()
    total = gathered(rows_all, yhi * 128, 128, 16)
    for g in range(8):
        half[g] = total[g * BPD : (g + 1) * BPD, :]
    p_copies = []
    for i, p in enumerate(xc_peers):
        to = lax.rem(xc + 1 + i, 8)
        p_copies.append(go(remote(half.at[to], parts.at[i], psend.at[i], precv.at[i], p)))

    lax.fori_loop(2, NREM, lambda s, v: (near_slot(s), v)[1], 0)

    near_all[8, 6:7, :] = ids_of(lambda s: within(stage[s]) + r * BPD, NNEAR)
    near_all[7, 6:7, :] = ids_of(lambda s: stage[NNEAR + s], NNEAR)
    c_copies = [
        go(remote(near_all.at[7], near_all.at[i], csend.at[i], crecv.at[i], p)) for i, p in enumerate(row_peers)
    ]
    for copy in f_copies:
        copy.wait_recv()
    acc = half[xc] + gathered(cols_all, r * BPD, BPD, 16)
    for i, copy in enumerate(p_copies):
        copy.wait_recv()
        acc = acc + parts[i]
    for copy in c_copies:
        copy.wait_recv()
    acc = acc + gathered(near_all, r * BPD, BPD, 6)
    for q in range(4):
        out[pl.ds(q, BPD, stride=4), :] = acc[:, q * 128 : (q + 1) * 128]
    for copy in started:
        copy.wait_send()

    def sent(s, _):
        for i in range(1, N_ROW):
            near_copy(i, s).wait_send()
        return 0

    lax.fori_loop(0, NREM, sent, 0)


def body(points, density, near_pairs, far_pairs, near_count, far_count):
    dma = pltpu.SemaphoreType.DMA
    smem = pl.BlockSpec(memory_space=pltpu.SMEM)
    hbm = pl.BlockSpec(memory_space=pltpu.HBM)
    out = pl.pallas_call(
        potential_kernel,
        out_shape=jax.ShapeDtypeStruct((BPD * 4, 128), F32),
        in_specs=[hbm, hbm, smem, smem, smem, smem],
        out_specs=pl.BlockSpec(memory_space=pltpu.VMEM),
        scratch_shapes=[
            pltpu.SMEM((N_ROW + 1, LIST), jnp.int32),
            pltpu.SMEM((LIST,), jnp.int32),
            vmem(BPD, 4, 4, BLK),
            vmem(BPD * 4, 128),
            vmem(8, 5, BPD, BLK),
            vmem(4, 5, BPD, BLK),
            vmem(BPD, BLK),
            vmem(5, NFAR, BLK),
            vmem(5, NFAR, BLK),
            vmem(5, NFAR, BLK),
            vmem(5, NFAR, BLK),
            vmem(5, NFAR, BLK),
            vmem(5, NFAR, BLK),
            vmem(N_ROW - 1, NREM, 4, 4, BLK),
            vmem(N_ROW - 1, 8, BLK),
            vmem(NREM, N_ROW, 4, 4, BLK),
            vmem(N_ROW, 8, BLK),
            vmem(128, BLK),
            vmem(128, BLK),
            vmem(NNEAR, BLK, 128, dtype=BF16),
            vmem(NNEAR, BLK, 128),
            vmem(NNEAR, 8, BLK),
            vmem(4, BLK, 128, dtype=BF16),
            vmem(4, 128, BLK, dtype=BF16),
            vmem(BLK, BLK),
            vmem(4, 4, BLK),
            vmem(32, BLK),
            vmem(32, BLK),
            vmem(2, 24, BLK),
            vmem(8, 24, BLK),
            vmem(9, 8, BLK),
            vmem(8, BPD, BLK),
            vmem(7, BPD, BLK),
            dma((BPD + 1,)),
            dma((8,)), dma((8,)), dma((7,)), dma((7,)), dma((3,)), dma((3,)),
            dma((7, NREM)), dma((7, NREM)), dma((7,)), dma((7,)), dma((2,)), dma((2,)),
            dma((1,)), dma((1,)), dma((7,)), dma((7,)), dma((7,)), dma((7,)), dma((7,)), dma((7,)),
        ],
        compiler_params=pltpu.CompilerParams(collective_id=0, has_side_effects=True, vmem_limit_bytes=64 << 20),
    )(points, density.reshape(-1, 128), near_pairs.T, far_pairs.T, near_count, far_count)
    return out.reshape(-1)


def solution(mesh):
    in_specs = (
        P(None, None, ("row", "col")),
        P(("row", "col")),
        P(("row", "col"), None),
        P(("row", "col"), None),
        P(("row", "col")),
        P(("row", "col")),
    )
    out_specs = P(("row", "col"))
    return jax.shard_map(body, mesh=mesh, in_specs=in_specs, out_specs=out_specs, check_vma=False)
```

```python
import jax
import jax.numpy as jnp
from jax import lax
from jax.experimental import pallas as pl
from jax.experimental.pallas import tpu as pltpu
from jax.sharding import PartitionSpec as P

BLK = 512
BPD = 16
NNEAR = 6
NFAR = 16
N_ROW = 8
N_COL = 16
soft_sq = 0.0004

MESH = pl.DeviceIdType.MESH
F32 = jnp.float32
BF16 = jnp.bfloat16
NREM = NNEAR - 1
LIST = 64


def vmem(*shape, dtype=F32):
    return pltpu.VMEM(shape, dtype)


def owner_of(block):
    return lax.shift_right_logical(block, 4)


def within(block):
    return block & (BPD - 1)


def row_mask(a, b, op):
    return op(jnp.full((1, BLK), a, jnp.int32), jnp.full((1, BLK), b, jnp.int32))


def same_rows(a, b):
    return row_mask(a, b, lambda x, y: x == y)


def split3(v):
    hi = v.astype(BF16).astype(F32)
    rest = v - hi
    mid = rest.astype(BF16).astype(F32)
    return hi, mid, rest - mid


def left_rows(px, py, pz, w):
    inv = 1.0 / (w * w)
    rows = []
    for v in ((px * px + py * py + pz * pz + soft_sq) * inv, inv, -2.0 * px * inv, -2.0 * py * inv, -2.0 * pz * inv):
        hi, mid, lo = split3(v)
        rows += [hi, hi, mid, mid, hi, lo]
    return rows


def right_rows(px, py, pz, w):
    inv = 1.0 / (w * w)
    rows = []
    for v in (inv, (px * px + py * py + pz * pz) * inv, px * inv, py * inv, pz * inv):
        hi, mid, lo = split3(v)
        rows += [hi, mid, hi, mid, lo, hi]
    return rows


def put_rows(ref, rows):
    n = rows[0].shape[0]
    for k, v in enumerate(rows):
        ref[k * n : (k + 1) * n, :] = v


def scatter(ids, base, count, vals):
    place = lax.broadcasted_iota(jnp.int32, (count, vals.shape[0]), 0) + base
    hot = jnp.where(place == ids, 1.0, 0.0).astype(BF16)
    out = None
    for part in split3(vals):
        v = jnp.dot(hot, part.astype(BF16), preferred_element_type=F32)
        out = v if out is None else out + v
    return out


def gathered(msgs, base, count, at):
    m, n, _ = msgs.shape
    ids = jnp.concatenate([msgs[i, at : at + 1, 0:n] for i in range(m)], axis=1).astype(jnp.int32)
    return scatter(ids, base, count, msgs[...].reshape(m * n, BLK))


def potential_kernel(
    pts_hbm, dens_hbm, npairs, fpairs, ncount, fcount,
    out,
    lists, stage, blocks, dens, cent_i, cent_j, own_dens, sel_i, sel_j, got_i, got_j, far_i, far_j,
    apack, agot, bpack, bgot, cpack, cgot,
    abuf, bbuf, left, turned, mids, lhs, rhs, tile, pj, fa, fb,
    rows_all, cols_far, near_all, half, parts, side, side_got,
    load, lsend, lrecv, xsend, xrecv, zsend, zrecv, asend, arecv, bsend, brecv, nsend, nrecv, ysend, yrecv,
    msend, mrecv, fsend, frecv, csend, crecv, psend, precv,
):
    r = lax.axis_index("row")
    c = lax.axis_index("col")
    z, ylo = r // 2, lax.rem(r, 2)
    yhi, xc = c // 8, lax.rem(c, 8)
    x, core = xc // 2, lax.rem(xc, 2)
    row_peers = [(lax.rem(r + i, N_ROW), c) for i in range(1, N_ROW)]
    xc_peers = [(r, yhi * 8 + lax.rem(xc + i, 8)) for i in range(1, 8)]
    x_up, x_down = [(r, yhi * 8 + lax.rem(x + i, 4) * 2 + core) for i in (1, 3)]
    zs = [lax.rem(z + i, 4) for i in range(4)]
    z_up, z_down = (zs[1] * 2 + ylo, c), (zs[3] * 2 + ylo, c)
    core_peer = (r, yhi * 8 + x * 2 + 1 - core)
    y_far = (r, lax.rem(c + 8, N_COL))
    y_near = (r + 1 - 2 * ylo, c)

    barrier = pltpu.get_barrier_semaphore()
    everyone = row_peers + xc_peers + [y_far]
    for p in everyone:
        pl.semaphore_signal(barrier, inc=1, device_id=p, device_id_type=MESH)

    loads = [
        pltpu.make_async_copy(pts_hbm.at[:, :, pl.ds(k * BLK, BLK)], blocks.at[k], load.at[k]) for k in range(BPD)
    ]
    loads.append(pltpu.make_async_copy(dens_hbm, dens, load.at[BPD]))
    for copy in loads:
        copy.start()

    for s in range(NNEAR):
        stage[s] = npairs[0, s]
        stage[NNEAR + s] = npairs[1, s]
        lists[r, NNEAR + s] = npairs[1, s]
    for s in range(NFAR):
        stage[16 + s] = fpairs[0, s]
        stage[32 + s] = fpairs[1, s]
    abuf[120:, :] = jnp.zeros((8, BLK), F32)
    bbuf[120:, :] = jnp.zeros((8, BLK), F32)
    fa[:, 32:, :] = jnp.zeros((2, 16, BLK), F32)
    fb[:, 30:, :] = jnp.zeros((2, 18, BLK), F32)
    sel_j[5] = jnp.zeros((NFAR, BLK), F32)
    for copy in loads:
        copy.wait()

    def centroid(k, _):
        p = blocks[k]
        w = p[3]
        total = jnp.sum(w, axis=0, keepdims=True)
        for d in range(3):
            cent_i[xc, d, pl.ds(k, 1), :] = jnp.sum(p[d] * w, axis=0, keepdims=True) / total
        cent_i[xc, 3, pl.ds(k, 1), :] = total
        return 0

    lax.fori_loop(0, BPD, centroid, 0)
    for q in range(4):
        own_dens[:, q * 128 : (q + 1) * 128] = dens[pl.ds(q, BPD, stride=4), :]
    cent_i[xc, 4] = own_dens[...]
    cent_j[z] = cent_i[xc]

    pl.semaphore_wait(barrier, len(everyone))

    def remote(src, dst, send, recv, peer):
        return pltpu.make_async_remote_copy(
            src_ref=src, dst_ref=dst, send_sem=send, recv_sem=recv, device_id=peer, device_id_type=MESH
        )

    started = []

    def go(copy):
        copy.start()
        started.append(copy)
        return copy

    list_copies = [go(remote(stage, lists.at[r], lsend.at[i], lrecv.at[i], p)) for i, p in enumerate(row_peers)]
    list_copies.append(go(remote(stage, lists.at[N_ROW], lsend.at[7], lrecv.at[7], y_far)))
    def ring(buf, index, up, down, send, recv):
        here, above, below = index(0), index(1), index(3)
        first = [
            go(remote(buf.at[here], buf.at[here], send.at[0], recv.at[0], up)),
            go(remote(buf.at[here], buf.at[here], send.at[1], recv.at[1], down)),
        ]

        def second():
            low, high = pl.ds(0, 8), pl.ds(8, 8)
            out = []
            first[0].wait_recv()
            out.append(go(remote(buf.at[below, :, low], buf.at[below, :, low], send.at[2], recv.at[2], up)))
            first[1].wait_recv()
            out.append(go(remote(buf.at[above, :, high], buf.at[above, :, high], send.at[3], recv.at[3], down)))
            return out

        return second

    def x_index(i):
        return lax.rem(x + i, 4) * 2 + core

    x_second = ring(cent_i, x_index, x_up, x_down, xsend, xrecv)
    z_second = ring(cent_j, lambda i: zs[i], z_up, z_down, zsend, zrecv)

    def to_core(i, sem):
        part = cent_i.at[x_index(i)]
        return go(remote(part, part, xsend.at[sem], xrecv.at[sem], core_peer))

    relays = [to_core(0, 4)]

    lane = lax.broadcasted_iota(jnp.int32, (BLK, 128), 1) % 4
    ri = lax.broadcasted_iota(jnp.int32, (128, 128), 0)
    ci = lax.broadcasted_iota(jnp.int32, (128, 128), 1)

    def spread(turned_rows, first):
        n = turned_rows.shape[1]
        k = lax.broadcasted_iota(jnp.int32, (n, 128), 0)
        pick = jnp.where((k >= first) & (k < first + 3), 1.0, 0.0).astype(BF16)
        return jnp.dot(turned_rows, pick, preferred_element_type=F32)

    def apply(halves, column, dj):
        part = None
        to_cols = []
        for q in range(4):
            blk = halves[q // 2][:, (q % 2) * 128 : (q % 2) * 128 + 128]
            e = blk * dj[:, q * 128 : (q + 1) * 128]
            part = e if part is None else part + e
            to_cols.append(jnp.sum(blk * column, axis=0, keepdims=True))
        to_rows = jnp.sum(jnp.transpose(part), axis=0, keepdims=True)
        return to_rows, jnp.concatenate(to_cols, axis=1)

    def masks(a, b, s, count):
        used = row_mask(s, count, lambda m, n: m < n)
        other = row_mask((b ^ (r * BPD + within(a))) | (owner_of(a) ^ c), 0, lambda m, n: m != n)
        return used, used & other

    def near_left(s, _):
        k = within(stage[s])
        p = blocks[k]
        mid = [jnp.mean(p[d]) for d in range(3)]
        put_rows(abuf, left_rows(*(p[d] - mid[d] for d in range(3)), p[3]))
        put_rows(abuf.at[120:123], split3(own_dens[pl.ds(k, 1), :]))
        at = jnp.transpose(abuf[...]).astype(BF16)
        left[s] = at
        turned[s] = spread(at, 120)
        for d in range(3):
            mids[s, d : d + 1, :] = jnp.full((1, BLK), mid[d], F32)
        return 0

    def near_right(s, p, dj):
        put_rows(bbuf, right_rows(*(p[d] - mids[s, d : d + 1, :] for d in range(3)), p[3]))
        bt = bbuf[...].astype(BF16)
        rhs[0] = bt
        for t in range(1, 4):
            shift = jnp.where((ri // 4 == ci // 4) & ((ri % 4 + t) % 4 == ci % 4), 1.0, 0.0).astype(BF16)
            rhs[t] = jnp.dot(shift, bt, preferred_element_type=F32).astype(BF16)
        at = left[s]
        for u in range(4):
            lhs[u] = jnp.where(lane == u, at, jnp.zeros_like(at))
        for t in range(4):
            for h in range(2):
                span = slice(h * 256, (h + 1) * 256)
                acc = None
                for u in range(4):
                    v = lax.rsqrt(jnp.dot(lhs[u], rhs[t][:, span], preferred_element_type=F32))
                    acc = v if acc is None else acc + v
                if t == 0:
                    tile[:, span] = acc
                else:
                    tile[:, span] += acc
        to_rows, to_cols = apply([tile.at[:, 0:256], tile.at[:, 256:512]], turned[s], dj)
        used, mirror = masks(stage[s], stage[NNEAR + s], s, ncount[0])
        near_all[8, pl.ds(s, 1), :] = jnp.where(used, to_rows, 0.0)
        near_all[7, pl.ds(s, 1), :] = jnp.where(mirror, to_cols, 0.0)

    def wanted(row, s):
        return lists[row, NNEAR + 1 + s]

    def item_mask(a, b):
        return jnp.full((4, 4, BLK), a, jnp.int32) == jnp.full((4, 4, BLK), b, jnp.int32)

    def a_copy(way, s):
        return remote(apack.at[s, way], agot.at[s, way], asend.at[way, s], arecv.at[way, s], (z_up, z_down)[way])

    def b_copy(way, s):
        return remote(bpack.at[s, way], bgot.at[s, way], bsend.at[way, s], brecv.at[way, s], (z_up, z_down)[way])

    def n_copy(s):
        return remote(cpack.at[s], cgot.at[s], nsend.at[s], nrecv.at[s], y_near)

    def step_a(s, _):
        for way in range(2):
            apack[s, way] = blocks[within(wanted(zs[2] * 2 + way, s))]
            a_copy(way, s).start()
        return 0

    def step_b(s, _):
        for way in range(2):
            to = zs[1 if way == 0 else 3] * 2
            bpack[s, way, 1 - way] = blocks[within(wanted(to + 1 - way, s))]
            b = wanted(to + way, s)
            a_copy(way, s).wait_recv()
            bpack[s, way, way] = jnp.where(item_mask(owner_of(b), r), blocks[within(b)], agot[s, way])
            b_copy(way, s).start()
        return 0

    def assembled(y, s):
        b = wanted(z * 2 + y, s)
        oz = lax.shift_right_logical(owner_of(b), 1)
        above = (oz ^ zs[1]) * ((oz ^ zs[2]) | (y ^ 1))
        v = jnp.where(item_mask(above, 0), bgot[s, 1, y], bgot[s, 0, y])
        return jnp.where(item_mask(oz, z), blocks[within(b)], v)

    def step_c(s, _):
        for way in range(2):
            b_copy(way, s).wait_recv()
        cpack[s] = assembled(1 - ylo, s)
        n_copy(s).start()
        return 0

    def near_slot(s):
        n_copy(s).wait_recv()
        b = stage[NNEAR + 1 + s]
        owner = owner_of(b)
        pj[...] = jnp.where(item_mask(owner & 1, ylo), assembled(ylo, s), cgot[s])
        here = cent_j[lax.shift_right_logical(owner, 1), 4, pl.ds(within(b), 1), :]
        d = jnp.where(same_rows(owner & 1, ylo), here, got_j[5, pl.ds(s, 1), :])
        near_right(s + 1, pj, d)

    for m in range(7, 9):
        near_all[m] = jnp.zeros((8, BLK), F32)
    lax.fori_loop(0, NNEAR, near_left, 0)

    for copy in list_copies:
        copy.wait_recv()
    lax.fori_loop(0, NREM, step_a, 0)
    x_half = x_second()
    z_half = z_second()
    relays += [to_core(3, 5), to_core(1, 6)]

    k0 = within(stage[0])
    pj[...] = blocks[k0]
    near_right(0, pj, own_dens[pl.ds(k0, 1), :])

    lax.fori_loop(0, NREM, step_b, 0)
    for copy in x_half:
        copy.wait_recv()
    relays.append(to_core(2, 7))
    for copy in z_half:
        copy.wait_recv()
    near_row = y_near[0]

    def choose_j(s, _):
        b = lists[near_row, 32 + s]
        g, k = lax.shift_right_logical(owner_of(b), 1), within(b)
        for f in range(5):
            sel_j[f, pl.ds(s, 1), :] = cent_j[g, f, pl.ds(k, 1), :]
        return 0

    lax.fori_loop(0, NFAR, choose_j, 0)
    for s in range(NREM):
        b = wanted(near_row, s)
        sel_j[5, s : s + 1, :] = cent_j[lax.shift_right_logical(owner_of(b), 1), 4, pl.ds(within(b), 1), :]
    yj_copy = go(remote(sel_j, got_j, ysend.at[1], yrecv.at[1], y_near))
    for copy in relays:
        copy.wait_recv()

    def choose_i(s, _):
        a = lists[N_ROW, 16 + s]
        g, k = owner_of(a) & 7, within(a)
        for f in range(5):
            sel_i[f, pl.ds(s, 1), :] = cent_i[g, f, pl.ds(k, 1), :]
        return 0

    lax.fori_loop(0, NFAR, choose_i, 0)
    yi_copy = go(remote(sel_i, got_i, ysend.at[0], yrecv.at[0], y_far))

    lax.fori_loop(0, 2, step_c, 0)
    yj_copy.wait_recv()
    near_slot(0)
    lax.fori_loop(2, NREM, step_c, 0)

    yi_copy.wait_recv()

    def take(s, _):
        a, b = stage[16 + s], stage[32 + s]
        owner, k = owner_of(a), within(a)
        here = same_rows(lax.shift_right_logical(owner, 3), yhi)
        one = pl.ds(s, 1)
        for f in range(5):
            far_i[f, one, :] = jnp.where(here, cent_i[owner & 7, f, pl.ds(k, 1), :], got_i[f, one, :])
        owner, k = owner_of(b), within(b)
        here = same_rows(owner & 1, ylo)
        for f in range(5):
            far_j[f, one, :] = jnp.where(
                here, cent_j[lax.shift_right_logical(owner, 1), f, pl.ds(k, 1), :], got_j[f, one, :]
            )
        return 0

    lax.fori_loop(0, NFAR, take, 0)
    for d in range(3):
        mid = jnp.mean(far_i[d], axis=1, keepdims=True)
        far_i[d] = far_i[d] - mid
        far_j[d] = far_j[d] - mid

    at_lane = lax.broadcasted_iota(jnp.int32, (1, BLK), 1)

    def ids_of(values, n):
        ids = jnp.full((1, BLK), -1, jnp.int32)
        for s in range(n):
            ids = jnp.where(at_lane == s, values(s), ids)
        return ids.astype(F32)

    for ref, first in ((rows_all.at[0], 16), (cols_far, 32)):
        ref[16:, :] = jnp.zeros((8, BLK), F32)
        ref[16:17, :] = ids_of(lambda s, first=first: stage[first + s], NFAR)

    def far(i, _):
        for n in range(2):
            s = 2 * i + n
            one = pl.ds(s, 1)
            put_rows(fa.at[n], left_rows(*(far_i[d, one, :] for d in range(4))) + list(split3(far_i[4, one, :])))
            put_rows(fb.at[n], right_rows(*(far_j[d, one, :] for d in range(4))))
            at = jnp.transpose(fa[n]).astype(BF16)
            bt = fb[n].astype(BF16)
            halves = [
                lax.rsqrt(jnp.dot(at, bt[:, h * 256 : (h + 1) * 256], preferred_element_type=F32)) for h in range(2)
            ]
            to_rows, to_cols = apply(halves, spread(at, 30), far_j[4, one, :])
            used, mirror = masks(stage[16 + s], stage[32 + s], s, fcount[0])
            rows_all[0, one, :] = jnp.where(used, to_rows, 0.0)
            cols_far[one, :] = jnp.where(mirror, to_cols, 0.0)
        return 0

    lax.fori_loop(0, NFAR // 2, far, 0)
    m_copy = go(remote(rows_all.at[0], rows_all.at[1], msend.at[0], mrecv.at[0], y_far))
    total = scatter(cols_far[16:17, 0:24].astype(jnp.int32), 0, 128, cols_far[...])
    for g in range(8):
        side[g] = total[g * BPD : (g + 1) * BPD, :]
    f_copies = [
        go(remote(side.at[lax.rem(r + 1 + i, N_ROW)], side_got.at[i], fsend.at[i], frecv.at[i], p))
        for i, p in enumerate(row_peers)
    ]

    near_slot(1)

    m_copy.wait_recv()
    total = gathered(rows_all, yhi * 128, 128, 16)
    for g in range(8):
        half[g] = total[g * BPD : (g + 1) * BPD, :]
    p_copies = []
    for i, p in enumerate(xc_peers):
        to = lax.rem(xc + 1 + i, 8)
        p_copies.append(go(remote(half.at[to], parts.at[i], psend.at[i], precv.at[i], p)))

    lax.fori_loop(2, NREM, lambda s, v: (near_slot(s), v)[1], 0)

    near_all[8, 6:7, :] = ids_of(lambda s: within(stage[s]) + r * BPD, NNEAR)
    near_all[7, 6:7, :] = ids_of(lambda s: stage[NNEAR + s], NNEAR)
    c_copies = [
        go(remote(near_all.at[7], near_all.at[i], csend.at[i], crecv.at[i], p)) for i, p in enumerate(row_peers)
    ]
    acc = half[xc] + side[r]
    for i, copy in enumerate(f_copies):
        copy.wait_recv()
        acc = acc + side_got[i]
    for i, copy in enumerate(p_copies):
        copy.wait_recv()
        acc = acc + parts[i]
    for copy in c_copies:
        copy.wait_recv()
    acc = acc + gathered(near_all, r * BPD, BPD, 6)
    for q in range(4):
        out[pl.ds(q, BPD, stride=4), :] = acc[:, q * 128 : (q + 1) * 128]
    for copy in started:
        copy.wait_send()

    def sent(s, _):
        for way in range(2):
            a_copy(way, s).wait_send()
            b_copy(way, s).wait_send()
        n_copy(s).wait_send()
        return 0

    lax.fori_loop(0, NREM, sent, 0)


def body(points, density, near_pairs, far_pairs, near_count, far_count):
    dma = pltpu.SemaphoreType.DMA
    smem = pl.BlockSpec(memory_space=pltpu.SMEM)
    hbm = pl.BlockSpec(memory_space=pltpu.HBM)
    out = pl.pallas_call(
        potential_kernel,
        out_shape=jax.ShapeDtypeStruct((BPD * 4, 128), F32),
        in_specs=[hbm, hbm, smem, smem, smem, smem],
        out_specs=pl.BlockSpec(memory_space=pltpu.VMEM),
        scratch_shapes=[
            pltpu.SMEM((N_ROW + 1, LIST), jnp.int32),
            pltpu.SMEM((LIST,), jnp.int32),
            vmem(BPD, 4, 4, BLK),
            vmem(BPD * 4, 128),
            vmem(8, 5, BPD, BLK),
            vmem(4, 5, BPD, BLK),
            vmem(BPD, BLK),
            vmem(5, NFAR, BLK),
            vmem(6, NFAR, BLK),
            vmem(5, NFAR, BLK),
            vmem(6, NFAR, BLK),
            vmem(5, NFAR, BLK),
            vmem(5, NFAR, BLK),
            vmem(NREM, 2, 4, 4, BLK),
            vmem(NREM, 2, 4, 4, BLK),
            vmem(NREM, 2, 2, 4, 4, BLK),
            vmem(NREM, 2, 2, 4, 4, BLK),
            vmem(NREM, 4, 4, BLK),
            vmem(NREM, 4, 4, BLK),
            vmem(128, BLK),
            vmem(128, BLK),
            vmem(NNEAR, BLK, 128, dtype=BF16),
            vmem(NNEAR, BLK, 128),
            vmem(NNEAR, 8, BLK),
            vmem(4, BLK, 128, dtype=BF16),
            vmem(4, 128, BLK, dtype=BF16),
            vmem(BLK, BLK),
            vmem(4, 4, BLK),
            vmem(2, 48, BLK),
            vmem(2, 48, BLK),
            vmem(2, 24, BLK),
            vmem(24, BLK),
            vmem(9, 8, BLK),
            vmem(8, BPD, BLK),
            vmem(7, BPD, BLK),
            vmem(8, BPD, BLK),
            vmem(7, BPD, BLK),
            dma((BPD + 1,)),
            dma((8,)), dma((8,)), dma((8,)), dma((8,)), dma((4,)), dma((4,)),
            dma((2, NREM)), dma((2, NREM)), dma((2, NREM)), dma((2, NREM)), dma((NREM,)), dma((NREM,)), dma((2,)), dma((2,)),
            dma((1,)), dma((1,)), dma((7,)), dma((7,)), dma((7,)), dma((7,)), dma((7,)), dma((7,)),
        ],
        compiler_params=pltpu.CompilerParams(collective_id=0, has_side_effects=True, vmem_limit_bytes=64 << 20),
    )(points, density.reshape(-1, 128), near_pairs.T, far_pairs.T, near_count, far_count)
    return out.reshape(-1)


def solution(mesh):
    in_specs = (
        P(None, None, ("row", "col")),
        P(("row", "col")),
        P(("row", "col"), None),
        P(("row", "col"), None),
        P(("row", "col")),
        P(("row", "col")),
    )
    out_specs = P(("row", "col"))
    return jax.shard_map(body, mesh=mesh, in_specs=in_specs, out_specs=out_specs, check_vma=False)
```

```python
import jax
import jax.numpy as jnp
from jax import lax
from jax.experimental import pallas as pl
from jax.experimental.pallas import tpu as pltpu
from jax.sharding import PartitionSpec as P

BLK = 512
BPD = 16
NNEAR = 6
NFAR = 16
N_ROW = 8
N_COL = 16
soft_sq = 0.0004

MESH = pl.DeviceIdType.MESH
F32 = jnp.float32
BF16 = jnp.bfloat16
NREM = NNEAR - 1
LIST = 64


def vmem(*shape, dtype=F32):
    return pltpu.VMEM(shape, dtype)


def owner_of(block):
    return lax.shift_right_logical(block, 4)


def within(block):
    return block & (BPD - 1)


def row_mask(a, b, op):
    return op(jnp.full((1, BLK), a, jnp.int32), jnp.full((1, BLK), b, jnp.int32))


def same_rows(a, b):
    return row_mask(a, b, lambda x, y: x == y)


def split3(v):
    hi = v.astype(BF16).astype(F32)
    rest = v - hi
    mid = rest.astype(BF16).astype(F32)
    return hi, mid, rest - mid


def left_rows(px, py, pz, w):
    inv = 1.0 / (w * w)
    rows = []
    for v in ((px * px + py * py + pz * pz + soft_sq) * inv, inv, -2.0 * px * inv, -2.0 * py * inv, -2.0 * pz * inv):
        hi, mid, lo = split3(v)
        rows += [hi, hi, mid, mid, hi, lo]
    return rows


def right_rows(px, py, pz, w):
    inv = 1.0 / (w * w)
    rows = []
    for v in (inv, (px * px + py * py + pz * pz) * inv, px * inv, py * inv, pz * inv):
        hi, mid, lo = split3(v)
        rows += [hi, mid, hi, mid, lo, hi]
    return rows


def put_rows(ref, rows):
    n = rows[0].shape[0]
    for k, v in enumerate(rows):
        ref[k * n : (k + 1) * n, :] = v


def scatter(ids, base, count, vals):
    place = lax.broadcasted_iota(jnp.int32, (count, vals.shape[0]), 0) + base
    hot = jnp.where(place == ids, 1.0, 0.0).astype(BF16)
    out = None
    for part in split3(vals):
        v = jnp.dot(hot, part.astype(BF16), preferred_element_type=F32)
        out = v if out is None else out + v
    return out


def gathered(msgs, base, count, at):
    m, n, _ = msgs.shape
    ids = jnp.concatenate([msgs[i, at : at + 1, 0:n] for i in range(m)], axis=1).astype(jnp.int32)
    return scatter(ids, base, count, msgs[...].reshape(m * n, BLK))


def potential_kernel(
    pts_hbm, dens_hbm, npairs, fpairs, ncount, fcount,
    out,
    lists, stage, blocks, dens, cent_i, cent_j, own_dens, sel_j, got_j, sel_d, got_d, far_i, far_j,
    apack, agot, bpack, bgot, cpack, cgot,
    abuf, bbuf, left, turned, mids, lhs, rhs, tile, pj, fa, fb,
    rows_all, cols_far, near_all, half, parts, side, side_got,
    load, lsend, lrecv, xsend, xrecv, zsend, zrecv, asend, arecv, bsend, brecv, nsend, nrecv, ysend, yrecv,
    msend, mrecv, fsend, frecv, csend, crecv, psend, precv,
):
    r = lax.axis_index("row")
    c = lax.axis_index("col")
    z, ylo = r // 2, lax.rem(r, 2)
    yhi, xc = c // 8, lax.rem(c, 8)
    x, core = xc // 2, lax.rem(xc, 2)
    row_peers = [(lax.rem(r + i, N_ROW), c) for i in range(1, N_ROW)]
    xc_peers = [(r, yhi * 8 + lax.rem(xc + i, 8)) for i in range(1, 8)]
    x_up, x_down = [(r, yhi * 8 + lax.rem(x + i, 4) * 2 + core) for i in (1, 3)]
    zs = [lax.rem(z + i, 4) for i in range(4)]
    z_up, z_down = (zs[1] * 2 + ylo, c), (zs[3] * 2 + ylo, c)
    core_peer = (r, yhi * 8 + x * 2 + 1 - core)
    y_far = (r, lax.rem(c + 8, N_COL))
    y_near = (r + 1 - 2 * ylo, c)

    barrier = pltpu.get_barrier_semaphore()
    everyone = row_peers + xc_peers + [y_far]
    for p in everyone:
        pl.semaphore_signal(barrier, inc=1, device_id=p, device_id_type=MESH)

    loads = [
        pltpu.make_async_copy(pts_hbm.at[:, :, pl.ds(k * BLK, BLK)], blocks.at[k], load.at[k]) for k in range(BPD)
    ]
    loads.append(pltpu.make_async_copy(dens_hbm, dens, load.at[BPD]))
    for copy in loads:
        copy.start()

    for s in range(NNEAR):
        stage[s] = npairs[0, s]
        stage[NNEAR + s] = npairs[1, s]
        lists[r, NNEAR + s] = npairs[1, s]
    for s in range(NFAR):
        stage[16 + s] = fpairs[0, s]
        stage[32 + s] = fpairs[1, s]
    abuf[120:, :] = jnp.zeros((8, BLK), F32)
    bbuf[120:, :] = jnp.zeros((8, BLK), F32)
    fa[:, 32:, :] = jnp.zeros((2, 16, BLK), F32)
    fb[:, 30:, :] = jnp.zeros((2, 18, BLK), F32)
    sel_d[...] = jnp.zeros((8, BLK), F32)
    for copy in loads:
        copy.wait()

    def centroid(k, _):
        p = blocks[k]
        w = p[3]
        total = jnp.sum(w, axis=0, keepdims=True)
        for d in range(3):
            cent_i[c, d, pl.ds(k, 1), :] = jnp.sum(p[d] * w, axis=0, keepdims=True) / total
        cent_i[c, 3, pl.ds(k, 1), :] = total
        return 0

    lax.fori_loop(0, BPD, centroid, 0)
    for q in range(4):
        own_dens[:, q * 128 : (q + 1) * 128] = dens[pl.ds(q, BPD, stride=4), :]
    cent_i[c, 4] = own_dens[...]
    cent_j[z] = cent_i[c]

    pl.semaphore_wait(barrier, len(everyone))

    def remote(src, dst, send, recv, peer):
        return pltpu.make_async_remote_copy(
            src_ref=src, dst_ref=dst, send_sem=send, recv_sem=recv, device_id=peer, device_id_type=MESH
        )

    started = []

    def go(copy):
        copy.start()
        started.append(copy)
        return copy

    list_copies = [go(remote(stage, lists.at[r], lsend.at[i], lrecv.at[i], p)) for i, p in enumerate(row_peers)]
    def ring(buf, index, up, down, send, recv):
        here, above, below = index(0), index(1), index(3)
        first = [
            go(remote(buf.at[here], buf.at[here], send.at[0], recv.at[0], up)),
            go(remote(buf.at[here], buf.at[here], send.at[1], recv.at[1], down)),
        ]

        def second():
            low, high = pl.ds(0, 8), pl.ds(8, 8)
            out = []
            first[0].wait_recv()
            out.append(go(remote(buf.at[below, :, low], buf.at[below, :, low], send.at[2], recv.at[2], up)))
            first[1].wait_recv()
            out.append(go(remote(buf.at[above, :, high], buf.at[above, :, high], send.at[3], recv.at[3], down)))
            return out

        return second

    def x_index(i, side):
        return (yhi if side == 0 else 1 - yhi) * 8 + lax.rem(x + i, 4) * 2 + core

    def x_ring(side):
        return ring(cent_i, lambda i: x_index(i, side), x_up, x_down, xsend.at[side], xrecv.at[side])

    relays = []

    def to_core(side, i):
        part = cent_i.at[x_index(i, side)]
        relays.append(go(remote(part, part, xsend.at[side, 4 + i], xrecv.at[side, 4 + i], core_peer)))

    yi_copy = go(remote(cent_i.at[c], cent_i.at[c], ysend.at[0], yrecv.at[0], y_far))
    x_second = x_ring(0)
    z_second = ring(cent_j, lambda i: zs[i], z_up, z_down, zsend, zrecv)
    to_core(0, 0)

    lane = lax.broadcasted_iota(jnp.int32, (BLK, 128), 1) % 4
    ri = lax.broadcasted_iota(jnp.int32, (128, 128), 0)
    ci = lax.broadcasted_iota(jnp.int32, (128, 128), 1)

    def spread(turned_rows, first):
        n = turned_rows.shape[1]
        k = lax.broadcasted_iota(jnp.int32, (n, 128), 0)
        pick = jnp.where((k >= first) & (k < first + 3), 1.0, 0.0).astype(BF16)
        return jnp.dot(turned_rows, pick, preferred_element_type=F32)

    def apply(halves, column, dj):
        part = None
        to_cols = []
        for q in range(4):
            blk = halves[q // 2][:, (q % 2) * 128 : (q % 2) * 128 + 128]
            e = blk * dj[:, q * 128 : (q + 1) * 128]
            part = e if part is None else part + e
            to_cols.append(jnp.sum(blk * column, axis=0, keepdims=True))
        to_rows = jnp.sum(jnp.transpose(part), axis=0, keepdims=True)
        return to_rows, jnp.concatenate(to_cols, axis=1)

    def masks(a, b, s, count):
        used = row_mask(s, count, lambda m, n: m < n)
        other = row_mask((b ^ (r * BPD + within(a))) | (owner_of(a) ^ c), 0, lambda m, n: m != n)
        return used, used & other

    def near_left(s, _):
        k = within(stage[s])
        p = blocks[k]
        mid = [jnp.mean(p[d]) for d in range(3)]
        put_rows(abuf, left_rows(*(p[d] - mid[d] for d in range(3)), p[3]))
        put_rows(abuf.at[120:123], split3(own_dens[pl.ds(k, 1), :]))
        at = jnp.transpose(abuf[...]).astype(BF16)
        left[s] = at
        turned[s] = spread(at, 120)
        for d in range(3):
            mids[s, d : d + 1, :] = jnp.full((1, BLK), mid[d], F32)
        return 0

    def near_right(s, p, dj):
        put_rows(bbuf, right_rows(*(p[d] - mids[s, d : d + 1, :] for d in range(3)), p[3]))
        bt = bbuf[...].astype(BF16)
        rhs[0] = bt
        for t in range(1, 4):
            shift = jnp.where((ri // 4 == ci // 4) & ((ri % 4 + t) % 4 == ci % 4), 1.0, 0.0).astype(BF16)
            rhs[t] = jnp.dot(shift, bt, preferred_element_type=F32).astype(BF16)
        at = left[s]
        for u in range(4):
            lhs[u] = jnp.where(lane == u, at, jnp.zeros_like(at))
        for t in range(4):
            for h in range(2):
                span = slice(h * 256, (h + 1) * 256)
                acc = None
                for u in range(4):
                    v = lax.rsqrt(jnp.dot(lhs[u], rhs[t][:, span], preferred_element_type=F32))
                    acc = v if acc is None else acc + v
                if t == 0:
                    tile[:, span] = acc
                else:
                    tile[:, span] += acc
        to_rows, to_cols = apply([tile.at[:, 0:256], tile.at[:, 256:512]], turned[s], dj)
        used, mirror = masks(stage[s], stage[NNEAR + s], s, ncount[0])
        near_all[8, pl.ds(s, 1), :] = jnp.where(used, to_rows, 0.0)
        near_all[7, pl.ds(s, 1), :] = jnp.where(mirror, to_cols, 0.0)

    def wanted(row, s):
        return lists[row, NNEAR + 1 + s]

    def item_mask(a, b):
        return jnp.full((4, 4, BLK), a, jnp.int32) == jnp.full((4, 4, BLK), b, jnp.int32)

    def a_copy(way, s):
        return remote(apack.at[s, way], agot.at[s, way], asend.at[way, s], arecv.at[way, s], (z_up, z_down)[way])

    def b_copy(way, s):
        return remote(bpack.at[s, way], bgot.at[s, way], bsend.at[way, s], brecv.at[way, s], (z_up, z_down)[way])

    def n_copy(s):
        return remote(cpack.at[s], cgot.at[s], nsend.at[s], nrecv.at[s], y_near)

    def step_a(s, _):
        for way in range(2):
            apack[s, way] = blocks[within(wanted(zs[2] * 2 + way, s))]
            a_copy(way, s).start()
        return 0

    def step_b(s, _):
        for way in range(2):
            to = zs[1 if way == 0 else 3] * 2
            bpack[s, way, 1 - way] = blocks[within(wanted(to + 1 - way, s))]
            b = wanted(to + way, s)
            a_copy(way, s).wait_recv()
            bpack[s, way, way] = jnp.where(item_mask(owner_of(b), r), blocks[within(b)], agot[s, way])
            b_copy(way, s).start()
        return 0

    def assembled(y, s):
        b = wanted(z * 2 + y, s)
        oz = lax.shift_right_logical(owner_of(b), 1)
        above = (oz ^ zs[1]) * ((oz ^ zs[2]) | (y ^ 1))
        v = jnp.where(item_mask(above, 0), bgot[s, 1, y], bgot[s, 0, y])
        return jnp.where(item_mask(oz, z), blocks[within(b)], v)

    def step_c(s, _):
        for way in range(2):
            b_copy(way, s).wait_recv()
        cpack[s] = assembled(1 - ylo, s)
        n_copy(s).start()
        return 0

    def near_slot(s):
        n_copy(s).wait_recv()
        b = stage[NNEAR + 1 + s]
        owner = owner_of(b)
        pj[...] = jnp.where(item_mask(owner & 1, ylo), assembled(ylo, s), cgot[s])
        here = cent_j[lax.shift_right_logical(owner, 1), 4, pl.ds(within(b), 1), :]
        d = jnp.where(same_rows(owner & 1, ylo), here, got_d[pl.ds(s, 1), :])
        near_right(s + 1, pj, d)

    for m in range(7, 9):
        near_all[m] = jnp.zeros((8, BLK), F32)
    lax.fori_loop(0, NNEAR, near_left, 0)

    for copy in list_copies:
        copy.wait_recv()
    lax.fori_loop(0, NREM, step_a, 0)
    x_half = x_second()
    z_half = z_second()
    to_core(0, 3)
    to_core(0, 1)
    lax.fori_loop(0, NREM, step_b, 0)
    yi_copy.wait_recv()
    x_second = x_ring(1)
    to_core(1, 0)

    k0 = within(stage[0])
    pj[...] = blocks[k0]
    near_right(0, pj, own_dens[pl.ds(k0, 1), :])

    for copy in z_half:
        copy.wait_recv()
    near_row = y_near[0]
    for s in range(NREM):
        b = wanted(near_row, s)
        sel_d[s : s + 1, :] = cent_j[lax.shift_right_logical(owner_of(b), 1), 4, pl.ds(within(b), 1), :]
    yd_copy = go(remote(sel_d, got_d, ysend.at[2], yrecv.at[2], y_near))
    lax.fori_loop(0, 1, step_c, 0)

    def choose_j(s, _):
        b = lists[near_row, 32 + s]
        g, k = lax.shift_right_logical(owner_of(b), 1), within(b)
        for f in range(5):
            sel_j[f, pl.ds(s, 1), :] = cent_j[g, f, pl.ds(k, 1), :]
        return 0

    lax.fori_loop(0, NFAR, choose_j, 0)
    yj_copy = go(remote(sel_j, got_j, ysend.at[1], yrecv.at[1], y_near))
    for copy in x_half:
        copy.wait_recv()
    to_core(0, 2)
    x_half = x_second()
    to_core(1, 3)
    to_core(1, 1)
    lax.fori_loop(1, 2, step_c, 0)
    yd_copy.wait_recv()
    near_slot(0)
    for copy in x_half:
        copy.wait_recv()
    to_core(1, 2)
    lax.fori_loop(2, NREM, step_c, 0)
    near_slot(1)

    yj_copy.wait_recv()
    for copy in relays:
        copy.wait_recv()

    def take(s, _):
        a, b = stage[16 + s], stage[32 + s]
        one = pl.ds(s, 1)
        for f in range(5):
            far_i[f, one, :] = cent_i[owner_of(a), f, pl.ds(within(a), 1), :]
        owner, k = owner_of(b), within(b)
        here = same_rows(owner & 1, ylo)
        for f in range(5):
            far_j[f, one, :] = jnp.where(
                here, cent_j[lax.shift_right_logical(owner, 1), f, pl.ds(k, 1), :], got_j[f, one, :]
            )
        return 0

    lax.fori_loop(0, NFAR, take, 0)
    for d in range(3):
        mid = jnp.mean(far_i[d], axis=1, keepdims=True)
        far_i[d] = far_i[d] - mid
        far_j[d] = far_j[d] - mid

    at_lane = lax.broadcasted_iota(jnp.int32, (1, BLK), 1)

    def ids_of(values, n):
        ids = jnp.full((1, BLK), -1, jnp.int32)
        for s in range(n):
            ids = jnp.where(at_lane == s, values(s), ids)
        return ids.astype(F32)

    for ref, first in ((rows_all.at[0], 16), (cols_far, 32)):
        ref[16:, :] = jnp.zeros((8, BLK), F32)
        ref[16:17, :] = ids_of(lambda s, first=first: stage[first + s], NFAR)

    def far(i, _):
        for n in range(2):
            s = 2 * i + n
            one = pl.ds(s, 1)
            put_rows(fa.at[n], left_rows(*(far_i[d, one, :] for d in range(4))) + list(split3(far_i[4, one, :])))
            put_rows(fb.at[n], right_rows(*(far_j[d, one, :] for d in range(4))))
            at = jnp.transpose(fa[n]).astype(BF16)
            bt = fb[n].astype(BF16)
            halves = [
                lax.rsqrt(jnp.dot(at, bt[:, h * 256 : (h + 1) * 256], preferred_element_type=F32)) for h in range(2)
            ]
            to_rows, to_cols = apply(halves, spread(at, 30), far_j[4, one, :])
            used, mirror = masks(stage[16 + s], stage[32 + s], s, fcount[0])
            rows_all[0, one, :] = jnp.where(used, to_rows, 0.0)
            cols_far[one, :] = jnp.where(mirror, to_cols, 0.0)
        return 0

    lax.fori_loop(0, NFAR // 2, far, 0)
    m_copy = go(remote(rows_all.at[0], rows_all.at[1], msend.at[0], mrecv.at[0], y_far))
    total = scatter(cols_far[16:17, 0:24].astype(jnp.int32), 0, 128, cols_far[...])
    for g in range(8):
        side[g] = total[g * BPD : (g + 1) * BPD, :]
    f_copies = [
        go(remote(side.at[lax.rem(r + 1 + i, N_ROW)], side_got.at[i], fsend.at[i], frecv.at[i], p))
        for i, p in enumerate(row_peers)
    ]

    near_slot(2)

    m_copy.wait_recv()
    total = gathered(rows_all, yhi * 128, 128, 16)
    for g in range(8):
        half[g] = total[g * BPD : (g + 1) * BPD, :]
    p_copies = []
    for i, p in enumerate(xc_peers):
        to = lax.rem(xc + 1 + i, 8)
        p_copies.append(go(remote(half.at[to], parts.at[i], psend.at[i], precv.at[i], p)))

    lax.fori_loop(3, NREM, lambda s, v: (near_slot(s), v)[1], 0)

    near_all[8, 6:7, :] = ids_of(lambda s: within(stage[s]) + r * BPD, NNEAR)
    near_all[7, 6:7, :] = ids_of(lambda s: stage[NNEAR + s], NNEAR)
    c_copies = [
        go(remote(near_all.at[7], near_all.at[i], csend.at[i], crecv.at[i], p)) for i, p in enumerate(row_peers)
    ]
    acc = half[xc] + side[r]
    for i, copy in enumerate(f_copies):
        copy.wait_recv()
        acc = acc + side_got[i]
    for i, copy in enumerate(p_copies):
        copy.wait_recv()
        acc = acc + parts[i]
    for copy in c_copies:
        copy.wait_recv()
    acc = acc + gathered(near_all, r * BPD, BPD, 6)
    for q in range(4):
        out[pl.ds(q, BPD, stride=4), :] = acc[:, q * 128 : (q + 1) * 128]
    for copy in started:
        copy.wait_send()

    def sent(s, _):
        for way in range(2):
            a_copy(way, s).wait_send()
            b_copy(way, s).wait_send()
        n_copy(s).wait_send()
        return 0

    lax.fori_loop(0, NREM, sent, 0)


def body(points, density, near_pairs, far_pairs, near_count, far_count):
    dma = pltpu.SemaphoreType.DMA
    smem = pl.BlockSpec(memory_space=pltpu.SMEM)
    hbm = pl.BlockSpec(memory_space=pltpu.HBM)
    out = pl.pallas_call(
        potential_kernel,
        out_shape=jax.ShapeDtypeStruct((BPD * 4, 128), F32),
        in_specs=[hbm, hbm, smem, smem, smem, smem],
        out_specs=pl.BlockSpec(memory_space=pltpu.VMEM),
        scratch_shapes=[
            pltpu.SMEM((N_ROW, LIST), jnp.int32),
            pltpu.SMEM((LIST,), jnp.int32),
            vmem(BPD, 4, 4, BLK),
            vmem(BPD * 4, 128),
            vmem(N_COL, 5, BPD, BLK),
            vmem(4, 5, BPD, BLK),
            vmem(BPD, BLK),
            vmem(5, NFAR, BLK),
            vmem(5, NFAR, BLK),
            vmem(8, BLK),
            vmem(8, BLK),
            vmem(5, NFAR, BLK),
            vmem(5, NFAR, BLK),
            vmem(NREM, 2, 4, 4, BLK),
            vmem(NREM, 2, 4, 4, BLK),
            vmem(NREM, 2, 2, 4, 4, BLK),
            vmem(NREM, 2, 2, 4, 4, BLK),
            vmem(NREM, 4, 4, BLK),
            vmem(NREM, 4, 4, BLK),
            vmem(128, BLK),
            vmem(128, BLK),
            vmem(NNEAR, BLK, 128, dtype=BF16),
            vmem(NNEAR, BLK, 128),
            vmem(NNEAR, 8, BLK),
            vmem(4, BLK, 128, dtype=BF16),
            vmem(4, 128, BLK, dtype=BF16),
            vmem(BLK, BLK),
            vmem(4, 4, BLK),
            vmem(2, 48, BLK),
            vmem(2, 48, BLK),
            vmem(2, 24, BLK),
            vmem(24, BLK),
            vmem(9, 8, BLK),
            vmem(8, BPD, BLK),
            vmem(7, BPD, BLK),
            vmem(8, BPD, BLK),
            vmem(7, BPD, BLK),
            dma((BPD + 1,)),
            dma((7,)), dma((7,)), dma((2, 8)), dma((2, 8)), dma((4,)), dma((4,)),
            dma((2, NREM)), dma((2, NREM)), dma((2, NREM)), dma((2, NREM)), dma((NREM,)), dma((NREM,)), dma((3,)), dma((3,)),
            dma((1,)), dma((1,)), dma((7,)), dma((7,)), dma((7,)), dma((7,)), dma((7,)), dma((7,)),
        ],
        compiler_params=pltpu.CompilerParams(collective_id=0, has_side_effects=True, vmem_limit_bytes=64 << 20),
    )(points, density.reshape(-1, 128), near_pairs.T, far_pairs.T, near_count, far_count)
    return out.reshape(-1)


def solution(mesh):
    in_specs = (
        P(None, None, ("row", "col")),
        P(("row", "col")),
        P(("row", "col"), None),
        P(("row", "col"), None),
        P(("row", "col")),
        P(("row", "col")),
    )
    out_specs = P(("row", "col"))
    return jax.shard_map(body, mesh=mesh, in_specs=in_specs, out_specs=out_specs, check_vma=False)
```

```python
import jax
import jax.numpy as jnp
from jax import lax
from jax.experimental import pallas as pl
from jax.experimental.pallas import tpu as pltpu
from jax.sharding import PartitionSpec as P

BLK = 512
BPD = 16
NNEAR = 6
NFAR = 16
N_ROW = 8
N_COL = 16
soft_sq = 0.0004

MESH = pl.DeviceIdType.MESH
F32 = jnp.float32
BF16 = jnp.bfloat16
NREM = NNEAR - 1
LIST = 64


def vmem(*shape, dtype=F32):
    return pltpu.VMEM(shape, dtype)


def owner_of(block):
    return lax.shift_right_logical(block, 4)


def within(block):
    return block & (BPD - 1)


def row_mask(a, b, op):
    return op(jnp.full((1, BLK), a, jnp.int32), jnp.full((1, BLK), b, jnp.int32))


def same_rows(a, b):
    return row_mask(a, b, lambda x, y: x == y)


def split3(v):
    hi = v.astype(BF16).astype(F32)
    rest = v - hi
    mid = rest.astype(BF16).astype(F32)
    return hi, mid, rest - mid


def left_rows(px, py, pz, w):
    inv = 1.0 / (w * w)
    rows = []
    for v in ((px * px + py * py + pz * pz + soft_sq) * inv, inv, -2.0 * px * inv, -2.0 * py * inv, -2.0 * pz * inv):
        hi, mid, lo = split3(v)
        rows += [hi, hi, mid, mid, hi, lo]
    return rows


def right_rows(px, py, pz, w):
    inv = 1.0 / (w * w)
    rows = []
    for v in (inv, (px * px + py * py + pz * pz) * inv, px * inv, py * inv, pz * inv):
        hi, mid, lo = split3(v)
        rows += [hi, mid, hi, mid, lo, hi]
    return rows


def put_rows(ref, rows):
    n = rows[0].shape[0]
    for k, v in enumerate(rows):
        ref[k * n : (k + 1) * n, :] = v


def scatter(ids, base, count, vals):
    place = lax.broadcasted_iota(jnp.int32, (count, vals.shape[0]), 0) + base
    hot = jnp.where(place == ids, 1.0, 0.0).astype(BF16)
    out = None
    for part in split3(vals):
        v = jnp.dot(hot, part.astype(BF16), preferred_element_type=F32)
        out = v if out is None else out + v
    return out


def gathered(msgs, base, count, at):
    m, n, _ = msgs.shape
    ids = jnp.concatenate([msgs[i, at : at + 1, 0:n] for i in range(m)], axis=1).astype(jnp.int32)
    return scatter(ids, base, count, msgs[...].reshape(m * n, BLK))


def potential_kernel(
    pts_hbm, dens_hbm, npairs, fpairs, ncount_hbm, fcount_hbm,
    out,
    ncount, fcount, lists, stage, blocks, dens, cent_i, cent_j, own_dens, sel_j, got_j, sel_d, got_d, far_i, far_j,
    apack, agot, bpack, bgot, cpack, cgot,
    abuf, bbuf, turned, mids, lhs, rhs, tile, pj, fa, fb, fd, fat, fbt, fdt,
    rows_all, cols_far, near_all, half, parts, side, side_got,
    load, lsend, lrecv, xsend, xrecv, zsend, zrecv, asend, arecv, bsend, brecv, nsend, nrecv, ysend, yrecv,
    msend, mrecv, fsend, frecv, csend, crecv, psend, precv,
):
    r = lax.axis_index("row")
    c = lax.axis_index("col")
    z, ylo = r // 2, lax.rem(r, 2)
    yhi, xc = c // 8, lax.rem(c, 8)
    x, core = xc // 2, lax.rem(xc, 2)
    row_peers = [(lax.rem(r + i, N_ROW), c) for i in range(1, N_ROW)]
    xc_peers = [(r, yhi * 8 + lax.rem(xc + i, 8)) for i in range(1, 8)]
    x_up, x_down = [(r, yhi * 8 + lax.rem(x + i, 4) * 2 + core) for i in (1, 3)]
    zs = [lax.rem(z + i, 4) for i in range(4)]
    z_up, z_down = (zs[1] * 2 + ylo, c), (zs[3] * 2 + ylo, c)
    core_peer = (r, yhi * 8 + x * 2 + 1 - core)
    y_far = (r, lax.rem(c + 8, N_COL))
    y_near = (r + 1 - 2 * ylo, c)

    barrier = pltpu.get_barrier_semaphore()
    everyone = row_peers + xc_peers + [y_far]
    for p in everyone:
        pl.semaphore_signal(barrier, inc=1, device_id=p, device_id_type=MESH)

    loads = [
        pltpu.make_async_copy(pts_hbm.at[:, :, pl.ds(k * BLK, BLK)], blocks.at[k], load.at[k]) for k in range(BPD)
    ]
    loads.append(pltpu.make_async_copy(dens_hbm, dens, load.at[BPD]))
    loads.append(pltpu.make_async_copy(ncount_hbm, ncount, load.at[BPD + 1]))
    loads.append(pltpu.make_async_copy(fcount_hbm, fcount, load.at[BPD + 2]))
    for copy in loads:
        copy.start()

    for s in range(NNEAR):
        stage[s] = npairs[0, s]
        stage[NNEAR + s] = npairs[1, s]
        lists[r, NNEAR + s] = npairs[1, s]
    for s in range(NFAR):
        stage[16 + s] = fpairs[0, s]
        stage[32 + s] = fpairs[1, s]
    abuf[120:, :] = jnp.zeros((8, BLK), F32)
    bbuf[120:, :] = jnp.zeros((8, BLK), F32)
    fa[240:, :] = jnp.zeros((16, BLK), F32)
    fb[240:, :] = jnp.zeros((16, BLK), F32)
    fd[24:, :] = jnp.zeros((8, BLK), F32)
    sel_d[...] = jnp.zeros((8, BLK), F32)
    for copy in loads:
        copy.wait()

    def centroid(k, _):
        p = blocks[k]
        w = p[3]
        total = jnp.sum(w, axis=0, keepdims=True)
        for d in range(3):
            cent_i[c, d, pl.ds(k, 1), :] = jnp.sum(p[d] * w, axis=0, keepdims=True) / total
        cent_i[c, 3, pl.ds(k, 1), :] = total
        return 0

    lax.fori_loop(0, BPD, centroid, 0)
    for q in range(4):
        own_dens[:, q * 128 : (q + 1) * 128] = dens[pl.ds(q, BPD, stride=4), :]
    cent_i[c, 4] = own_dens[...]
    cent_j[z] = cent_i[c]

    pl.semaphore_wait(barrier, len(everyone))

    def remote(src, dst, send, recv, peer):
        return pltpu.make_async_remote_copy(
            src_ref=src, dst_ref=dst, send_sem=send, recv_sem=recv, device_id=peer, device_id_type=MESH
        )

    started = []

    def go(copy):
        copy.start()
        started.append(copy)
        return copy

    list_copies = [go(remote(stage, lists.at[r], lsend.at[i], lrecv.at[i], p)) for i, p in enumerate(row_peers)]
    def ring(buf, index, up, down, send, recv):
        here, above, below = index(0), index(1), index(3)
        first = [
            go(remote(buf.at[here], buf.at[here], send.at[0], recv.at[0], up)),
            go(remote(buf.at[here], buf.at[here], send.at[1], recv.at[1], down)),
        ]

        def second():
            low, high = pl.ds(0, 8), pl.ds(8, 8)
            out = []
            first[0].wait_recv()
            out.append(go(remote(buf.at[below, :, low], buf.at[below, :, low], send.at[2], recv.at[2], up)))
            first[1].wait_recv()
            out.append(go(remote(buf.at[above, :, high], buf.at[above, :, high], send.at[3], recv.at[3], down)))
            return out

        return second

    def x_index(i, side):
        return (yhi if side == 0 else 1 - yhi) * 8 + lax.rem(x + i, 4) * 2 + core

    def x_ring(side):
        return ring(cent_i, lambda i: x_index(i, side), x_up, x_down, xsend.at[side], xrecv.at[side])

    relays = []

    def to_core(side, i):
        part = cent_i.at[x_index(i, side)]
        relays.append(go(remote(part, part, xsend.at[side, 4 + i], xrecv.at[side, 4 + i], core_peer)))

    yi_copy = go(remote(cent_i.at[c], cent_i.at[c], ysend.at[0], yrecv.at[0], y_far))
    x_second = x_ring(0)
    z_second = ring(cent_j, lambda i: zs[i], z_up, z_down, zsend, zrecv)
    to_core(0, 0)

    lane = lax.broadcasted_iota(jnp.int32, (BLK, 128), 1) % 4
    ri = lax.broadcasted_iota(jnp.int32, (128, 128), 0)
    ci = lax.broadcasted_iota(jnp.int32, (128, 128), 1)

    def spread(turned_rows, chosen):
        k = lax.broadcasted_iota(jnp.int32, (turned_rows.shape[1], 128), 0)
        return jnp.dot(turned_rows, jnp.where(chosen(k), 1.0, 0.0).astype(BF16), preferred_element_type=F32)

    def apply(halves, column, dj):
        part = None
        to_cols = []
        for q in range(4):
            blk = halves[q // 2][:, (q % 2) * 128 : (q % 2) * 128 + 128]
            e = blk * dj[:, q * 128 : (q + 1) * 128]
            part = e if part is None else part + e
            to_cols.append(jnp.sum(blk * column, axis=0, keepdims=True))
        to_rows = jnp.sum(jnp.transpose(part), axis=0, keepdims=True)
        return to_rows, jnp.concatenate(to_cols, axis=1)

    def masks(a, b, s, count):
        used = row_mask(s, count, lambda m, n: m < n)
        other = row_mask((b ^ (r * BPD + within(a))) | (owner_of(a) ^ c), 0, lambda m, n: m != n)
        return used, used & other

    def near_left(s, _):
        k = within(stage[s])
        p = blocks[k]
        mid = [jnp.mean(p[d]) for d in range(3)]
        put_rows(abuf, left_rows(*(p[d] - mid[d] for d in range(3)), p[3]))
        put_rows(abuf.at[120:123], split3(own_dens[pl.ds(k, 1), :]))
        at = jnp.transpose(abuf[...]).astype(BF16)
        for u in range(4):
            lhs[s, u] = jnp.where(lane == u, at, jnp.zeros_like(at))
        turned[s] = spread(at, lambda k: (k >= 120) & (k < 123))
        for d in range(3):
            mids[s, d : d + 1, :] = jnp.full((1, BLK), mid[d], F32)
        return 0

    def near_right(s, p, dj):
        put_rows(bbuf, right_rows(*(p[d] - mids[s, d : d + 1, :] for d in range(3)), p[3]))
        bt = bbuf[...].astype(BF16)
        rhs[0] = bt
        for t in range(1, 4):
            shift = jnp.where((ri // 4 == ci // 4) & ((ri % 4 + t) % 4 == ci % 4), 1.0, 0.0).astype(BF16)
            rhs[t] = jnp.dot(shift, bt, preferred_element_type=F32).astype(BF16)
        for t in range(4):
            for h in range(2):
                span = slice(h * 256, (h + 1) * 256)
                acc = None
                for u in range(4):
                    v = lax.rsqrt(jnp.dot(lhs[s, u], rhs[t][:, span], preferred_element_type=F32))
                    acc = v if acc is None else acc + v
                if t == 0:
                    tile[:, span] = acc
                else:
                    tile[:, span] += acc
        to_rows, to_cols = apply([tile.at[:, 0:256], tile.at[:, 256:512]], turned[s], dj)
        used, mirror = masks(stage[s], stage[NNEAR + s], s, ncount[0])
        near_all[8, pl.ds(s, 1), :] = jnp.where(used, to_rows, 0.0)
        near_all[7, pl.ds(s, 1), :] = jnp.where(mirror, to_cols, 0.0)

    def wanted(row, s):
        return lists[row, NNEAR + 1 + s]

    def item_mask(a, b):
        return jnp.full((4, 4, BLK), a, jnp.int32) == jnp.full((4, 4, BLK), b, jnp.int32)

    def a_copy(way, s):
        return remote(apack.at[s, way], agot.at[s, way], asend.at[way, s], arecv.at[way, s], (z_up, z_down)[way])

    def b_copy(way, s):
        return remote(bpack.at[s, way], bgot.at[s, way], bsend.at[way, s], brecv.at[way, s], (z_up, z_down)[way])

    def n_copy(s):
        return remote(cpack.at[s], cgot.at[s], nsend.at[s], nrecv.at[s], y_near)

    def step_a(s, _):
        for way in range(2):
            apack[s, way] = blocks[within(wanted(zs[2] * 2 + way, s))]
            a_copy(way, s).start()
        return 0

    def step_b(s, _):
        for way in range(2):
            to = zs[1 if way == 0 else 3] * 2
            bpack[s, way, 1 - way] = blocks[within(wanted(to + 1 - way, s))]
            b = wanted(to + way, s)
            a_copy(way, s).wait_recv()
            bpack[s, way, way] = jnp.where(item_mask(owner_of(b), r), blocks[within(b)], agot[s, way])
            b_copy(way, s).start()
        return 0

    def assembled(y, s):
        b = wanted(z * 2 + y, s)
        oz = lax.shift_right_logical(owner_of(b), 1)
        above = (oz ^ zs[1]) * ((oz ^ zs[2]) | (y ^ 1))
        v = jnp.where(item_mask(above, 0), bgot[s, 1, y], bgot[s, 0, y])
        return jnp.where(item_mask(oz, z), blocks[within(b)], v)

    def step_c(s, _):
        for way in range(2):
            b_copy(way, s).wait_recv()
        cpack[s] = assembled(1 - ylo, s)
        n_copy(s).start()
        return 0

    def near_slot(s):
        n_copy(s).wait_recv()
        b = stage[NNEAR + 1 + s]
        owner = owner_of(b)
        pj[...] = jnp.where(item_mask(owner & 1, ylo), assembled(ylo, s), cgot[s])
        here = cent_j[lax.shift_right_logical(owner, 1), 4, pl.ds(within(b), 1), :]
        d = jnp.where(same_rows(owner & 1, ylo), here, got_d[pl.ds(s, 1), :])
        near_right(s + 1, pj, d)

    for m in range(7, 9):
        near_all[m] = jnp.zeros((8, BLK), F32)
    lax.fori_loop(0, 2, near_left, 0)

    for copy in list_copies:
        copy.wait_recv()
    lax.fori_loop(0, NREM, step_a, 0)
    x_half = x_second()
    z_half = z_second()
    to_core(0, 3)
    to_core(0, 1)

    k0 = within(stage[0])
    pj[...] = blocks[k0]
    near_right(0, pj, own_dens[pl.ds(k0, 1), :])

    lax.fori_loop(0, NREM, step_b, 0)
    yi_copy.wait_recv()
    x_second = x_ring(1)
    to_core(1, 0)
    lax.fori_loop(2, NNEAR, near_left, 0)
    for copy in x_half:
        copy.wait_recv()
    to_core(0, 2)

    for copy in z_half:
        copy.wait_recv()
    near_row = y_near[0]
    for s in range(NREM):
        b = wanted(near_row, s)
        sel_d[s : s + 1, :] = cent_j[lax.shift_right_logical(owner_of(b), 1), 4, pl.ds(within(b), 1), :]
    yd_copy = go(remote(sel_d, got_d, ysend.at[2], yrecv.at[2], y_near))

    def choose_j(s, _):
        b = lists[near_row, 32 + s]
        g, k = lax.shift_right_logical(owner_of(b), 1), within(b)
        for f in range(5):
            sel_j[f, pl.ds(s, 1), :] = cent_j[g, f, pl.ds(k, 1), :]
        return 0

    lax.fori_loop(0, NFAR, choose_j, 0)
    yj_copy = go(remote(sel_j, got_j, ysend.at[1], yrecv.at[1], y_near))
    lax.fori_loop(0, 2, step_c, 0)
    x_half = x_second()
    to_core(1, 3)
    to_core(1, 1)
    yd_copy.wait_recv()
    near_slot(0)
    for copy in x_half:
        copy.wait_recv()
    to_core(1, 2)
    lax.fori_loop(2, NREM, step_c, 0)
    near_slot(1)

    yj_copy.wait_recv()
    for copy in relays:
        copy.wait_recv()

    def take(s, _):
        a, b = stage[16 + s], stage[32 + s]
        one = pl.ds(s, 1)
        for f in range(5):
            far_i[f, one, :] = cent_i[owner_of(a), f, pl.ds(within(a), 1), :]
        owner, k = owner_of(b), within(b)
        here = same_rows(owner & 1, ylo)
        for f in range(5):
            far_j[f, one, :] = jnp.where(
                here, cent_j[lax.shift_right_logical(owner, 1), f, pl.ds(k, 1), :], got_j[f, one, :]
            )
        return 0

    lax.fori_loop(0, NFAR, take, 0)
    for d in range(3):
        mid = jnp.mean(far_i[d], axis=1, keepdims=True)
        far_i[d] = far_i[d] - mid
        far_j[d] = far_j[d] - mid

    at_lane = lax.broadcasted_iota(jnp.int32, (1, BLK), 1)

    def ids_of(values, n):
        ids = jnp.full((1, BLK), -1, jnp.int32)
        for s in range(n):
            ids = jnp.where(at_lane == s, values(s), ids)
        return ids.astype(F32)

    for ref, first in ((rows_all.at[0], 16), (cols_far, 32)):
        ref[16:, :] = jnp.zeros((8, BLK), F32)
        ref[16:17, :] = ids_of(lambda s, first=first: stage[first + s], NFAR)

    for g in range(2):
        eight = slice(g * 8, g * 8 + 8)
        put_rows(fa, left_rows(*(far_i[d, eight, :] for d in range(4))))
        put_rows(fb, right_rows(*(far_j[d, eight, :] for d in range(4))))
        put_rows(fd, split3(far_i[4, eight, :]))
        fat[g] = jnp.transpose(fa[...]).astype(BF16)
        fbt[g] = fb[...].astype(BF16)
        fdt[g] = jnp.transpose(fd[...]).astype(BF16)
    far_lane = lax.broadcasted_iota(jnp.int32, (BLK, 256), 1) % 8

    def far(i, _):
        for n in range(2):
            s = 2 * i + n
            g, e = s // 8, lax.rem(s, 8)
            one = pl.ds(s, 1)
            at = fat[g]
            at = jnp.where(far_lane == e, at, jnp.zeros_like(at))
            halves = [
                lax.rsqrt(jnp.dot(at, fbt[g, :, h * 256 : (h + 1) * 256], preferred_element_type=F32))
                for h in range(2)
            ]
            column = spread(fdt[g], lambda k, e=e: (k % 8 == e) & (k < 24))
            to_rows, to_cols = apply(halves, column, far_j[4, one, :])
            used, mirror = masks(stage[16 + s], stage[32 + s], s, fcount[0])
            rows_all[0, one, :] = jnp.where(used, to_rows, 0.0)
            cols_far[one, :] = jnp.where(mirror, to_cols, 0.0)
        return 0

    lax.fori_loop(0, NFAR // 2, far, 0)
    m_copy = go(remote(rows_all.at[0], rows_all.at[1], msend.at[0], mrecv.at[0], y_far))
    total = scatter(cols_far[16:17, 0:24].astype(jnp.int32), 0, 128, cols_far[...])
    for g in range(8):
        side[g] = total[g * BPD : (g + 1) * BPD, :]
    f_copies = [
        go(remote(side.at[lax.rem(r + 1 + i, N_ROW)], side_got.at[i], fsend.at[i], frecv.at[i], p))
        for i, p in enumerate(row_peers)
    ]

    lax.fori_loop(2, 4, lambda s, v: (near_slot(s), v)[1], 0)

    m_copy.wait_recv()
    total = gathered(rows_all, yhi * 128, 128, 16)
    for g in range(8):
        half[g] = total[g * BPD : (g + 1) * BPD, :]
    p_copies = []
    for i, p in enumerate(xc_peers):
        to = lax.rem(xc + 1 + i, 8)
        p_copies.append(go(remote(half.at[to], parts.at[i], psend.at[i], precv.at[i], p)))

    near_slot(4)

    near_all[8, 6:7, :] = ids_of(lambda s: within(stage[s]) + r * BPD, NNEAR)
    near_all[7, 6:7, :] = ids_of(lambda s: stage[NNEAR + s], NNEAR)
    c_copies = [
        go(remote(near_all.at[7], near_all.at[i], csend.at[i], crecv.at[i], p)) for i, p in enumerate(row_peers)
    ]
    acc = half[xc] + side[r]
    for i, copy in enumerate(f_copies):
        copy.wait_recv()
        acc = acc + side_got[i]
    for i, copy in enumerate(p_copies):
        copy.wait_recv()
        acc = acc + parts[i]
    for copy in c_copies:
        copy.wait_recv()
    acc = acc + gathered(near_all, r * BPD, BPD, 6)
    for q in range(4):
        out[pl.ds(q, BPD, stride=4), :] = acc[:, q * 128 : (q + 1) * 128]
    for copy in started:
        copy.wait_send()

    def sent(s, _):
        for way in range(2):
            a_copy(way, s).wait_send()
            b_copy(way, s).wait_send()
        n_copy(s).wait_send()
        return 0

    lax.fori_loop(0, NREM, sent, 0)


def body(points, density, near_pairs, far_pairs, near_count, far_count):
    dma = pltpu.SemaphoreType.DMA
    smem = pl.BlockSpec(memory_space=pltpu.SMEM)
    hbm = pl.BlockSpec(memory_space=pltpu.HBM)
    out = pl.pallas_call(
        potential_kernel,
        out_shape=jax.ShapeDtypeStruct((BPD * 4, 128), F32),
        in_specs=[hbm, hbm, smem, smem, hbm, hbm],
        out_specs=pl.BlockSpec(memory_space=pltpu.VMEM),
        scratch_shapes=[
            pltpu.SMEM((1,), jnp.int32),
            pltpu.SMEM((1,), jnp.int32),
            pltpu.SMEM((N_ROW, LIST), jnp.int32),
            pltpu.SMEM((LIST,), jnp.int32),
            vmem(BPD, 4, 4, BLK),
            vmem(BPD * 4, 128),
            vmem(N_COL, 5, BPD, BLK),
            vmem(4, 5, BPD, BLK),
            vmem(BPD, BLK),
            vmem(5, NFAR, BLK),
            vmem(5, NFAR, BLK),
            vmem(8, BLK),
            vmem(8, BLK),
            vmem(5, NFAR, BLK),
            vmem(5, NFAR, BLK),
            vmem(NREM, 2, 4, 4, BLK),
            vmem(NREM, 2, 4, 4, BLK),
            vmem(NREM, 2, 2, 4, 4, BLK),
            vmem(NREM, 2, 2, 4, 4, BLK),
            vmem(NREM, 4, 4, BLK),
            vmem(NREM, 4, 4, BLK),
            vmem(128, BLK),
            vmem(128, BLK),
            vmem(NNEAR, BLK, 128),
            vmem(NNEAR, 8, BLK),
            vmem(NNEAR, 4, BLK, 128, dtype=BF16),
            vmem(4, 128, BLK, dtype=BF16),
            vmem(BLK, BLK),
            vmem(4, 4, BLK),
            vmem(256, BLK),
            vmem(256, BLK),
            vmem(32, BLK),
            vmem(2, BLK, 256, dtype=BF16),
            vmem(2, 256, BLK, dtype=BF16),
            vmem(2, BLK, 32, dtype=BF16),
            vmem(2, 24, BLK),
            vmem(24, BLK),
            vmem(9, 8, BLK),
            vmem(8, BPD, BLK),
            vmem(7, BPD, BLK),
            vmem(8, BPD, BLK),
            vmem(7, BPD, BLK),
            dma((BPD + 3,)),
            dma((7,)), dma((7,)), dma((2, 8)), dma((2, 8)), dma((4,)), dma((4,)),
            dma((2, NREM)), dma((2, NREM)), dma((2, NREM)), dma((2, NREM)), dma((NREM,)), dma((NREM,)), dma((3,)), dma((3,)),
            dma((1,)), dma((1,)), dma((7,)), dma((7,)), dma((7,)), dma((7,)), dma((7,)), dma((7,)),
        ],
        compiler_params=pltpu.CompilerParams(collective_id=0, has_side_effects=True, vmem_limit_bytes=64 << 20),
    )(points, density.reshape(-1, 128), near_pairs.T, far_pairs.T, near_count, far_count)
    return out.reshape(-1)


def solution(mesh):
    in_specs = (
        P(None, None, ("row", "col")),
        P(("row", "col")),
        P(("row", "col"), None),
        P(("row", "col"), None),
        P(("row", "col")),
        P(("row", "col")),
    )
    out_specs = P(("row", "col"))
    return jax.shard_map(body, mesh=mesh, in_specs=in_specs, out_specs=out_specs, check_vma=False)
```

```python
import jax
import jax.numpy as jnp
from jax import lax
from jax.experimental import pallas as pl
from jax.experimental.pallas import tpu as pltpu
from jax.sharding import PartitionSpec as P

BLK = 512
BPD = 16
NNEAR = 6
NFAR = 16
N_ROW = 8
N_COL = 16
soft_sq = 0.0004

MESH = pl.DeviceIdType.MESH
F32 = jnp.float32
BF16 = jnp.bfloat16
NREM = NNEAR - 1
LIST = 64


def vmem(*shape, dtype=F32):
    return pltpu.VMEM(shape, dtype)


def owner_of(block):
    return lax.shift_right_logical(block, 4)


def within(block):
    return block & (BPD - 1)


def row_mask(a, b, op):
    return op(jnp.full((1, BLK), a, jnp.int32), jnp.full((1, BLK), b, jnp.int32))


def same_rows(a, b):
    return row_mask(a, b, lambda x, y: x == y)


def split3(v):
    hi = v.astype(BF16).astype(F32)
    rest = v - hi
    mid = rest.astype(BF16).astype(F32)
    return hi, mid, rest - mid


def left_rows(px, py, pz, w):
    inv = 1.0 / (w * w)
    rows = []
    for v in ((px * px + py * py + pz * pz + soft_sq) * inv, inv, -2.0 * px * inv, -2.0 * py * inv, -2.0 * pz * inv):
        hi, mid, lo = split3(v)
        rows += [hi, hi, mid, mid, hi, lo]
    return rows


def right_rows(px, py, pz, w):
    inv = 1.0 / (w * w)
    rows = []
    for v in (inv, (px * px + py * py + pz * pz) * inv, px * inv, py * inv, pz * inv):
        hi, mid, lo = split3(v)
        rows += [hi, mid, hi, mid, lo, hi]
    return rows


def put_rows(ref, rows):
    n = rows[0].shape[0]
    for k, v in enumerate(rows):
        ref[k * n : (k + 1) * n, :] = v


def scatter(ids, base, count, vals):
    place = lax.broadcasted_iota(jnp.int32, (count, vals.shape[0]), 0) + base
    hot = jnp.where(place == ids, 1.0, 0.0).astype(BF16)
    out = None
    for part in split3(vals):
        v = jnp.dot(hot, part.astype(BF16), preferred_element_type=F32)
        out = v if out is None else out + v
    return out


def gathered(msgs, base, count, at):
    m, n, _ = msgs.shape
    ids = jnp.concatenate([msgs[i, at : at + 1, 0:n] for i in range(m)], axis=1).astype(jnp.int32)
    return scatter(ids, base, count, msgs[...].reshape(m * n, BLK))


def potential_kernel(
    pts_hbm, dens_hbm, npairs, fpairs, ncount_hbm, fcount_hbm,
    out,
    ncount, fcount, lists, stage, blocks, dens, cent_i, cent_j, own_dens, sel_j, got_j, sel_d, got_d, far_i, far_j,
    apack, agot, bpack, bgot, cpack, cgot,
    abuf, bbuf, turned, mids, lhs, rhs, tile, pj, fa, fb, fd, fat, fbt, fdt,
    rows_all, cols_far, near_all, half, parts, side, side_got,
    load, lsend, lrecv, xsend, xrecv, zsend, zrecv, asend, arecv, bsend, brecv, nsend, nrecv, ysend, yrecv,
    msend, mrecv, fsend, frecv, csend, crecv, psend, precv,
):
    r = lax.axis_index("row")
    c = lax.axis_index("col")
    z, ylo = r // 2, lax.rem(r, 2)
    yhi, xc = c // 8, lax.rem(c, 8)
    x, core = xc // 2, lax.rem(xc, 2)
    row_peers = [(lax.rem(r + i, N_ROW), c) for i in range(1, N_ROW)]
    xc_peers = [(r, yhi * 8 + lax.rem(xc + i, 8)) for i in range(1, 8)]
    x_up, x_down = [(r, yhi * 8 + lax.rem(x + i, 4) * 2 + core) for i in (1, 3)]
    zs = [lax.rem(z + i, 4) for i in range(4)]
    z_up, z_down = (zs[1] * 2 + ylo, c), (zs[3] * 2 + ylo, c)
    core_peer = (r, yhi * 8 + x * 2 + 1 - core)
    y_far = (r, lax.rem(c + 8, N_COL))
    y_near = (r + 1 - 2 * ylo, c)

    barrier = pltpu.get_barrier_semaphore()
    everyone = row_peers + xc_peers + [y_far]
    for p in everyone:
        pl.semaphore_signal(barrier, inc=1, device_id=p, device_id_type=MESH)

    loads = [
        pltpu.make_async_copy(pts_hbm.at[:, :, pl.ds(k * BLK, BLK)], blocks.at[k], load.at[k]) for k in range(BPD)
    ]
    loads.append(pltpu.make_async_copy(dens_hbm, dens, load.at[BPD]))
    loads.append(pltpu.make_async_copy(ncount_hbm, ncount, load.at[BPD + 1]))
    loads.append(pltpu.make_async_copy(fcount_hbm, fcount, load.at[BPD + 2]))
    for copy in loads:
        copy.start()

    for s in range(NNEAR):
        stage[s] = npairs[0, s]
        stage[NNEAR + s] = npairs[1, s]
        lists[r, NNEAR + s] = npairs[1, s]
    for s in range(NFAR):
        stage[16 + s] = fpairs[0, s]
        stage[32 + s] = fpairs[1, s]
    abuf[120:, :] = jnp.zeros((8, BLK), F32)
    bbuf[120:, :] = jnp.zeros((8, BLK), F32)
    fa[240:, :] = jnp.zeros((16, BLK), F32)
    fb[240:, :] = jnp.zeros((16, BLK), F32)
    fd[24:, :] = jnp.zeros((8, BLK), F32)
    sel_d[...] = jnp.zeros((8, BLK), F32)
    for copy in loads:
        copy.wait()

    def centroid(k, _):
        p = blocks[k]
        w = p[3]
        total = jnp.sum(w, axis=0, keepdims=True)
        for d in range(3):
            cent_i[c, d, pl.ds(k, 1), :] = jnp.sum(p[d] * w, axis=0, keepdims=True) / total
        cent_i[c, 3, pl.ds(k, 1), :] = total
        return 0

    lax.fori_loop(0, BPD, centroid, 0)
    for q in range(4):
        own_dens[:, q * 128 : (q + 1) * 128] = dens[pl.ds(q, BPD, stride=4), :]
    cent_i[c, 4] = own_dens[...]
    cent_j[z] = cent_i[c]

    pl.semaphore_wait(barrier, len(everyone))

    def remote(src, dst, send, recv, peer):
        return pltpu.make_async_remote_copy(
            src_ref=src, dst_ref=dst, send_sem=send, recv_sem=recv, device_id=peer, device_id_type=MESH
        )

    started = []

    def go(copy):
        copy.start()
        started.append(copy)
        return copy

    list_copies = [go(remote(stage, lists.at[r], lsend.at[i], lrecv.at[i], p)) for i, p in enumerate(row_peers)]
    def ring(buf, index, up, down, send, recv):
        here, above, below = index(0), index(1), index(3)
        first = [
            go(remote(buf.at[here], buf.at[here], send.at[0], recv.at[0], up)),
            go(remote(buf.at[here], buf.at[here], send.at[1], recv.at[1], down)),
        ]

        def second():
            low, high = pl.ds(0, 8), pl.ds(8, 8)
            out = []
            first[0].wait_recv()
            out.append(go(remote(buf.at[below, :, low], buf.at[below, :, low], send.at[2], recv.at[2], up)))
            first[1].wait_recv()
            out.append(go(remote(buf.at[above, :, high], buf.at[above, :, high], send.at[3], recv.at[3], down)))
            return out

        return second

    def x_index(i, side):
        return (yhi if side == 0 else 1 - yhi) * 8 + lax.rem(x + i, 4) * 2 + core

    def x_ring(side):
        return ring(cent_i, lambda i: x_index(i, side), x_up, x_down, xsend.at[side], xrecv.at[side])

    relays = []

    def to_core(side, i):
        part = cent_i.at[x_index(i, side)]
        relays.append(go(remote(part, part, xsend.at[side, 4 + i], xrecv.at[side, 4 + i], core_peer)))

    yi_copy = go(remote(cent_i.at[c], cent_i.at[c], ysend.at[0], yrecv.at[0], y_far))
    x_second = x_ring(0)
    z_second = ring(cent_j, lambda i: zs[i], z_up, z_down, zsend, zrecv)
    to_core(0, 0)

    lane = lax.broadcasted_iota(jnp.int32, (BLK, 128), 1) % 4
    ri = lax.broadcasted_iota(jnp.int32, (128, 128), 0)
    ci = lax.broadcasted_iota(jnp.int32, (128, 128), 1)

    def spread(turned_rows, chosen):
        k = lax.broadcasted_iota(jnp.int32, (turned_rows.shape[1], 128), 0)
        return jnp.dot(turned_rows, jnp.where(chosen(k), 1.0, 0.0).astype(BF16), preferred_element_type=F32)

    def apply(halves, column, dj):
        part = None
        to_cols = []
        for q in range(4):
            blk = halves[q // 2][:, (q % 2) * 128 : (q % 2) * 128 + 128]
            e = blk * dj[:, q * 128 : (q + 1) * 128]
            part = e if part is None else part + e
            to_cols.append(jnp.sum(blk * column, axis=0, keepdims=True))
        to_rows = jnp.sum(jnp.transpose(part), axis=0, keepdims=True)
        return to_rows, jnp.concatenate(to_cols, axis=1)

    def masks(a, b, s, count):
        used = row_mask(s, count, lambda m, n: m < n)
        other = row_mask((b ^ (r * BPD + within(a))) | (owner_of(a) ^ c), 0, lambda m, n: m != n)
        return used, used & other

    def near_left(s, _):
        k = within(stage[s])
        p = blocks[k]
        mid = [jnp.mean(p[d]) for d in range(3)]
        put_rows(abuf, left_rows(*(p[d] - mid[d] for d in range(3)), p[3]))
        put_rows(abuf.at[120:123], split3(own_dens[pl.ds(k, 1), :]))
        at = jnp.transpose(abuf[...]).astype(BF16)
        for u in range(4):
            lhs[s, u] = jnp.where(lane == u, at, jnp.zeros_like(at))
        turned[s] = spread(at, lambda k: (k >= 120) & (k < 123))
        for d in range(3):
            mids[s, d : d + 1, :] = jnp.full((1, BLK), mid[d], F32)
        return 0

    def near_right(s, p, dj):
        put_rows(bbuf, right_rows(*(p[d] - mids[s, d : d + 1, :] for d in range(3)), p[3]))
        bt = bbuf[...].astype(BF16)
        rhs[0] = bt
        for t in range(1, 4):
            shift = jnp.where((ri // 4 == ci // 4) & ((ri % 4 + t) % 4 == ci % 4), 1.0, 0.0).astype(BF16)
            rhs[t] = jnp.dot(shift, bt, preferred_element_type=F32).astype(BF16)
        for h in range(2):
            span = slice(h * 256, (h + 1) * 256)
            for i in range(2):
                rows = slice(i * 256, (i + 1) * 256)
                acc = None
                for t in range(4):
                    for u in range(4):
                        v = lax.rsqrt(jnp.dot(lhs[s, u, rows, :], rhs[t][:, span], preferred_element_type=F32))
                        acc = v if acc is None else acc + v
                tile[rows, span] = acc
        to_rows, to_cols = apply([tile.at[:, 0:256], tile.at[:, 256:512]], turned[s], dj)
        used, mirror = masks(stage[s], stage[NNEAR + s], s, ncount[0])
        near_all[8, pl.ds(s, 1), :] = jnp.where(used, to_rows, 0.0)
        near_all[7, pl.ds(s, 1), :] = jnp.where(mirror, to_cols, 0.0)

    def wanted(row, s):
        return lists[row, NNEAR + 1 + s]

    def item_mask(a, b):
        return jnp.full((4, 4, BLK), a, jnp.int32) == jnp.full((4, 4, BLK), b, jnp.int32)

    def a_copy(way, s):
        return remote(apack.at[s, way], agot.at[s, way], asend.at[way, s], arecv.at[way, s], (z_up, z_down)[way])

    def b_copy(way, s):
        return remote(bpack.at[s, way], bgot.at[s, way], bsend.at[way, s], brecv.at[way, s], (z_up, z_down)[way])

    def n_copy(s):
        return remote(cpack.at[s], cgot.at[s], nsend.at[s], nrecv.at[s], y_near)

    def step_a(s, _):
        for way in range(2):
            apack[s, way] = blocks[within(wanted(zs[2] * 2 + way, s))]
            a_copy(way, s).start()
        return 0

    def step_b(s, _):
        for way in range(2):
            to = zs[1 if way == 0 else 3] * 2
            bpack[s, way, 1 - way] = blocks[within(wanted(to + 1 - way, s))]
            b = wanted(to + way, s)
            a_copy(way, s).wait_recv()
            bpack[s, way, way] = jnp.where(item_mask(owner_of(b), r), blocks[within(b)], agot[s, way])
            b_copy(way, s).start()
        return 0

    def assembled(y, s):
        b = wanted(z * 2 + y, s)
        oz = lax.shift_right_logical(owner_of(b), 1)
        above = (oz ^ zs[1]) * ((oz ^ zs[2]) | (y ^ 1))
        v = jnp.where(item_mask(above, 0), bgot[s, 1, y], bgot[s, 0, y])
        return jnp.where(item_mask(oz, z), blocks[within(b)], v)

    def step_c(s, _):
        for way in range(2):
            b_copy(way, s).wait_recv()
        cpack[s] = assembled(1 - ylo, s)
        n_copy(s).start()
        return 0

    def near_slot(s):
        n_copy(s).wait_recv()
        b = stage[NNEAR + 1 + s]
        owner = owner_of(b)
        pj[...] = jnp.where(item_mask(owner & 1, ylo), assembled(ylo, s), cgot[s])
        here = cent_j[lax.shift_right_logical(owner, 1), 4, pl.ds(within(b), 1), :]
        d = jnp.where(same_rows(owner & 1, ylo), here, got_d[pl.ds(s, 1), :])
        near_right(s + 1, pj, d)

    for m in range(7, 9):
        near_all[m] = jnp.zeros((8, BLK), F32)
    lax.fori_loop(0, 2, near_left, 0)

    for copy in list_copies:
        copy.wait_recv()
    lax.fori_loop(0, NREM, step_a, 0)
    x_half = x_second()
    z_half = z_second()
    to_core(0, 3)
    to_core(0, 1)

    k0 = within(stage[0])
    pj[...] = blocks[k0]
    near_right(0, pj, own_dens[pl.ds(k0, 1), :])

    lax.fori_loop(0, NREM, step_b, 0)
    yi_copy.wait_recv()
    x_second = x_ring(1)
    to_core(1, 0)
    lax.fori_loop(2, NNEAR, near_left, 0)
    for copy in x_half:
        copy.wait_recv()
    to_core(0, 2)

    for copy in z_half:
        copy.wait_recv()
    near_row = y_near[0]
    for s in range(NREM):
        b = wanted(near_row, s)
        sel_d[s : s + 1, :] = cent_j[lax.shift_right_logical(owner_of(b), 1), 4, pl.ds(within(b), 1), :]
    yd_copy = go(remote(sel_d, got_d, ysend.at[2], yrecv.at[2], y_near))

    def choose_j(s, _):
        b = lists[near_row, 32 + s]
        g, k = lax.shift_right_logical(owner_of(b), 1), within(b)
        for f in range(5):
            sel_j[f, pl.ds(s, 1), :] = cent_j[g, f, pl.ds(k, 1), :]
        return 0

    lax.fori_loop(0, NFAR, choose_j, 0)
    yj_copy = go(remote(sel_j, got_j, ysend.at[1], yrecv.at[1], y_near))
    lax.fori_loop(0, 2, step_c, 0)
    x_half = x_second()
    to_core(1, 3)
    to_core(1, 1)
    yd_copy.wait_recv()
    near_slot(0)
    for copy in x_half:
        copy.wait_recv()
    to_core(1, 2)
    lax.fori_loop(2, NREM, step_c, 0)
    near_slot(1)

    yj_copy.wait_recv()
    for copy in relays:
        copy.wait_recv()

    def take(s, _):
        a, b = stage[16 + s], stage[32 + s]
        one = pl.ds(s, 1)
        for f in range(5):
            far_i[f, one, :] = cent_i[owner_of(a), f, pl.ds(within(a), 1), :]
        owner, k = owner_of(b), within(b)
        here = same_rows(owner & 1, ylo)
        for f in range(5):
            far_j[f, one, :] = jnp.where(
                here, cent_j[lax.shift_right_logical(owner, 1), f, pl.ds(k, 1), :], got_j[f, one, :]
            )
        return 0

    lax.fori_loop(0, NFAR, take, 0)
    for d in range(3):
        mid = jnp.mean(far_i[d], axis=1, keepdims=True)
        far_i[d] = far_i[d] - mid
        far_j[d] = far_j[d] - mid

    at_lane = lax.broadcasted_iota(jnp.int32, (1, BLK), 1)

    def ids_of(values, n):
        ids = jnp.full((1, BLK), -1, jnp.int32)
        for s in range(n):
            ids = jnp.where(at_lane == s, values(s), ids)
        return ids.astype(F32)

    for ref, first in ((rows_all.at[0], 16), (cols_far, 32)):
        ref[16:, :] = jnp.zeros((8, BLK), F32)
        ref[16:17, :] = ids_of(lambda s, first=first: stage[first + s], NFAR)

    for g in range(2):
        eight = slice(g * 8, g * 8 + 8)
        put_rows(fa, left_rows(*(far_i[d, eight, :] for d in range(4))))
        put_rows(fb, right_rows(*(far_j[d, eight, :] for d in range(4))))
        put_rows(fd, split3(far_i[4, eight, :]))
        fat[g] = jnp.transpose(fa[...]).astype(BF16)
        fbt[g] = fb[...].astype(BF16)
        fdt[g] = jnp.transpose(fd[...]).astype(BF16)
    far_lane = lax.broadcasted_iota(jnp.int32, (BLK, 256), 1) % 8

    def far(i, _):
        for n in range(2):
            s = 2 * i + n
            g, e = s // 8, lax.rem(s, 8)
            one = pl.ds(s, 1)
            at = fat[g]
            at = jnp.where(far_lane == e, at, jnp.zeros_like(at))
            halves = [
                lax.rsqrt(jnp.dot(at, fbt[g, :, h * 256 : (h + 1) * 256], preferred_element_type=F32))
                for h in range(2)
            ]
            column = spread(fdt[g], lambda k, e=e: (k % 8 == e) & (k < 24))
            to_rows, to_cols = apply(halves, column, far_j[4, one, :])
            used, mirror = masks(stage[16 + s], stage[32 + s], s, fcount[0])
            rows_all[0, one, :] = jnp.where(used, to_rows, 0.0)
            cols_far[one, :] = jnp.where(mirror, to_cols, 0.0)
        return 0

    lax.fori_loop(0, NFAR // 2, far, 0)
    m_copy = go(remote(rows_all.at[0], rows_all.at[1], msend.at[0], mrecv.at[0], y_far))
    total = scatter(cols_far[16:17, 0:24].astype(jnp.int32), 0, 128, cols_far[...])
    for g in range(8):
        side[g] = total[g * BPD : (g + 1) * BPD, :]
    f_copies = [
        go(remote(side.at[lax.rem(r + 1 + i, N_ROW)], side_got.at[i], fsend.at[i], frecv.at[i], p))
        for i, p in enumerate(row_peers)
    ]

    lax.fori_loop(2, 4, lambda s, v: (near_slot(s), v)[1], 0)

    m_copy.wait_recv()
    total = gathered(rows_all, yhi * 128, 128, 16)
    for g in range(8):
        half[g] = total[g * BPD : (g + 1) * BPD, :]
    p_copies = []
    for i, p in enumerate(xc_peers):
        to = lax.rem(xc + 1 + i, 8)
        p_copies.append(go(remote(half.at[to], parts.at[i], psend.at[i], precv.at[i], p)))

    near_slot(4)

    near_all[8, 6:7, :] = ids_of(lambda s: within(stage[s]) + r * BPD, NNEAR)
    near_all[7, 6:7, :] = ids_of(lambda s: stage[NNEAR + s], NNEAR)
    c_copies = [
        go(remote(near_all.at[7], near_all.at[i], csend.at[i], crecv.at[i], p)) for i, p in enumerate(row_peers)
    ]
    acc = half[xc] + side[r]
    for i, copy in enumerate(f_copies):
        copy.wait_recv()
        acc = acc + side_got[i]
    for i, copy in enumerate(p_copies):
        copy.wait_recv()
        acc = acc + parts[i]
    for copy in c_copies:
        copy.wait_recv()
    acc = acc + gathered(near_all, r * BPD, BPD, 6)
    for q in range(4):
        out[pl.ds(q, BPD, stride=4), :] = acc[:, q * 128 : (q + 1) * 128]
    for copy in started:
        copy.wait_send()

    def sent(s, _):
        for way in range(2):
            a_copy(way, s).wait_send()
            b_copy(way, s).wait_send()
        n_copy(s).wait_send()
        return 0

    lax.fori_loop(0, NREM, sent, 0)


def body(points, density, near_pairs, far_pairs, near_count, far_count):
    dma = pltpu.SemaphoreType.DMA
    smem = pl.BlockSpec(memory_space=pltpu.SMEM)
    hbm = pl.BlockSpec(memory_space=pltpu.HBM)
    out = pl.pallas_call(
        potential_kernel,
        out_shape=jax.ShapeDtypeStruct((BPD * 4, 128), F32),
        in_specs=[hbm, hbm, smem, smem, hbm, hbm],
        out_specs=pl.BlockSpec(memory_space=pltpu.VMEM),
        scratch_shapes=[
            pltpu.SMEM((1,), jnp.int32),
            pltpu.SMEM((1,), jnp.int32),
            pltpu.SMEM((N_ROW, LIST), jnp.int32),
            pltpu.SMEM((LIST,), jnp.int32),
            vmem(BPD, 4, 4, BLK),
            vmem(BPD * 4, 128),
            vmem(N_COL, 5, BPD, BLK),
            vmem(4, 5, BPD, BLK),
            vmem(BPD, BLK),
            vmem(5, NFAR, BLK),
            vmem(5, NFAR, BLK),
            vmem(8, BLK),
            vmem(8, BLK),
            vmem(5, NFAR, BLK),
            vmem(5, NFAR, BLK),
            vmem(NREM, 2, 4, 4, BLK),
            vmem(NREM, 2, 4, 4, BLK),
            vmem(NREM, 2, 2, 4, 4, BLK),
            vmem(NREM, 2, 2, 4, 4, BLK),
            vmem(NREM, 4, 4, BLK),
            vmem(NREM, 4, 4, BLK),
            vmem(128, BLK),
            vmem(128, BLK),
            vmem(NNEAR, BLK, 128),
            vmem(NNEAR, 8, BLK),
            vmem(NNEAR, 4, BLK, 128, dtype=BF16),
            vmem(4, 128, BLK, dtype=BF16),
            vmem(BLK, BLK),
            vmem(4, 4, BLK),
            vmem(256, BLK),
            vmem(256, BLK),
            vmem(32, BLK),
            vmem(2, BLK, 256, dtype=BF16),
            vmem(2, 256, BLK, dtype=BF16),
            vmem(2, BLK, 32, dtype=BF16),
            vmem(2, 24, BLK),
            vmem(24, BLK),
            vmem(9, 8, BLK),
            vmem(8, BPD, BLK),
            vmem(7, BPD, BLK),
            vmem(8, BPD, BLK),
            vmem(7, BPD, BLK),
            dma((BPD + 3,)),
            dma((7,)), dma((7,)), dma((2, 8)), dma((2, 8)), dma((4,)), dma((4,)),
            dma((2, NREM)), dma((2, NREM)), dma((2, NREM)), dma((2, NREM)), dma((NREM,)), dma((NREM,)), dma((3,)), dma((3,)),
            dma((1,)), dma((1,)), dma((7,)), dma((7,)), dma((7,)), dma((7,)), dma((7,)), dma((7,)),
        ],
        compiler_params=pltpu.CompilerParams(collective_id=0, has_side_effects=True, vmem_limit_bytes=64 << 20),
    )(points, density.reshape(-1, 128), near_pairs.T, far_pairs.T, near_count, far_count)
    return out.reshape(-1)


def solution(mesh):
    in_specs = (
        P(None, None, ("row", "col")),
        P(("row", "col")),
        P(("row", "col"), None),
        P(("row", "col"), None),
        P(("row", "col")),
        P(("row", "col")),
    )
    out_specs = P(("row", "col"))
    return jax.shard_map(body, mesh=mesh, in_specs=in_specs, out_specs=out_specs, check_vma=False)
```

```python
import jax
import jax.numpy as jnp
from jax import lax
from jax.experimental import pallas as pl
from jax.experimental.pallas import tpu as pltpu
from jax.sharding import PartitionSpec as P

BLK = 512
BPD = 16
NNEAR = 6
NFAR = 16
N_ROW = 8
N_COL = 16
soft_sq = 0.0004

MESH = pl.DeviceIdType.MESH
F32 = jnp.float32
BF16 = jnp.bfloat16
NREM = NNEAR - 1
LIST = 64


def vmem(*shape, dtype=F32):
    return pltpu.VMEM(shape, dtype)


def owner_of(block):
    return lax.shift_right_logical(block, 4)


def within(block):
    return block & (BPD - 1)


def row_mask(a, b, op):
    return op(jnp.full((1, BLK), a, jnp.int32), jnp.full((1, BLK), b, jnp.int32))


def same_rows(a, b):
    return row_mask(a, b, lambda x, y: x == y)


def split3(v):
    hi = v.astype(BF16).astype(F32)
    rest = v - hi
    mid = rest.astype(BF16).astype(F32)
    return hi, mid, rest - mid


def left_rows(px, py, pz, w):
    inv = 1.0 / (w * w)
    rows = []
    for v in ((px * px + py * py + pz * pz + soft_sq) * inv, inv, -2.0 * px * inv, -2.0 * py * inv, -2.0 * pz * inv):
        hi, mid, lo = split3(v)
        rows += [hi, hi, mid, mid, hi, lo]
    return rows


def right_rows(px, py, pz, w):
    inv = 1.0 / (w * w)
    rows = []
    for v in (inv, (px * px + py * py + pz * pz) * inv, px * inv, py * inv, pz * inv):
        hi, mid, lo = split3(v)
        rows += [hi, mid, hi, mid, lo, hi]
    return rows


def put_rows(ref, rows):
    n = rows[0].shape[0]
    for k, v in enumerate(rows):
        ref[k * n : (k + 1) * n, :] = v


def scatter(ids, base, count, vals):
    place = lax.broadcasted_iota(jnp.int32, (count, vals.shape[0]), 0) + base
    hot = jnp.where(place == ids, 1.0, 0.0).astype(BF16)
    out = None
    for part in split3(vals):
        v = jnp.dot(hot, part.astype(BF16), preferred_element_type=F32)
        out = v if out is None else out + v
    return out


def gathered(msgs, base, count, at):
    m, n, _ = msgs.shape
    ids = jnp.concatenate([msgs[i, at : at + 1, 0:n] for i in range(m)], axis=1).astype(jnp.int32)
    return scatter(ids, base, count, msgs[...].reshape(m * n, BLK))


def potential_kernel(
    pts_hbm, dens_hbm, npairs, fpairs, ncount_hbm, fcount_hbm,
    out,
    ncount, fcount, lists, stage, blocks, dens, cent_i, cent_j, own_dens, sel_j, got_j, sel_d, got_d, far_i, far_j,
    apack, agot, bpack, bgot, cpack, cgot,
    abuf, bbuf, turned, mids, lhs, rhs, tile, pj, fa, fb, fd, fat, fbt, fdt,
    rows_all, cols_far, near_all, half, parts, side, side_got,
    load, lsend, lrecv, xsend, xrecv, zsend, zrecv, asend, arecv, bsend, brecv, nsend, nrecv, ysend, yrecv,
    msend, mrecv, fsend, frecv, csend, crecv, psend, precv,
):
    r = lax.axis_index("row")
    c = lax.axis_index("col")
    z, ylo = r // 2, lax.rem(r, 2)
    yhi, xc = c // 8, lax.rem(c, 8)
    x, core = xc // 2, lax.rem(xc, 2)
    row_peers = [(lax.rem(r + i, N_ROW), c) for i in range(1, N_ROW)]
    xc_peers = [(r, yhi * 8 + lax.rem(xc + i, 8)) for i in range(1, 8)]
    x_up, x_down = [(r, yhi * 8 + lax.rem(x + i, 4) * 2 + core) for i in (1, 3)]
    zs = [lax.rem(z + i, 4) for i in range(4)]
    z_up, z_down = (zs[1] * 2 + ylo, c), (zs[3] * 2 + ylo, c)
    core_peer = (r, yhi * 8 + x * 2 + 1 - core)
    y_far = (r, lax.rem(c + 8, N_COL))
    y_near = (r + 1 - 2 * ylo, c)

    barrier = pltpu.get_barrier_semaphore()
    everyone = row_peers + xc_peers + [y_far]
    for p in everyone:
        pl.semaphore_signal(barrier, inc=1, device_id=p, device_id_type=MESH)

    loads = [
        pltpu.make_async_copy(pts_hbm.at[:, :, pl.ds(k * BLK, BLK)], blocks.at[k], load.at[k]) for k in range(BPD)
    ]
    loads.append(pltpu.make_async_copy(dens_hbm, dens, load.at[BPD]))
    loads.append(pltpu.make_async_copy(ncount_hbm, ncount, load.at[BPD + 1]))
    loads.append(pltpu.make_async_copy(fcount_hbm, fcount, load.at[BPD + 2]))
    for copy in loads:
        copy.start()

    for s in range(NNEAR):
        stage[s] = npairs[0, s]
        stage[NNEAR + s] = npairs[1, s]
        lists[r, NNEAR + s] = npairs[1, s]
    for s in range(NFAR):
        stage[16 + s] = fpairs[0, s]
        stage[32 + s] = fpairs[1, s]
    abuf[120:, :] = jnp.zeros((8, BLK), F32)
    bbuf[120:, :] = jnp.zeros((8, BLK), F32)
    fa[240:, :] = jnp.zeros((16, BLK), F32)
    fb[240:, :] = jnp.zeros((16, BLK), F32)
    fd[24:, :] = jnp.zeros((8, BLK), F32)
    sel_d[...] = jnp.zeros((8, BLK), F32)
    for copy in loads:
        copy.wait()

    def centroid(k, _):
        p = blocks[k]
        w = p[3]
        total = jnp.sum(w, axis=0, keepdims=True)
        for d in range(3):
            cent_i[c, d, pl.ds(k, 1), :] = jnp.sum(p[d] * w, axis=0, keepdims=True) / total
        cent_i[c, 3, pl.ds(k, 1), :] = total
        return 0

    lax.fori_loop(0, BPD, centroid, 0)
    for q in range(4):
        own_dens[:, q * 128 : (q + 1) * 128] = dens[pl.ds(q, BPD, stride=4), :]
    cent_i[c, 4] = own_dens[...]
    cent_j[z] = cent_i[c]

    pl.semaphore_wait(barrier, len(everyone))

    def remote(src, dst, send, recv, peer):
        return pltpu.make_async_remote_copy(
            src_ref=src, dst_ref=dst, send_sem=send, recv_sem=recv, device_id=peer, device_id_type=MESH
        )

    started = []

    def go(copy):
        copy.start()
        started.append(copy)
        return copy

    list_copies = [go(remote(stage, lists.at[r], lsend.at[i], lrecv.at[i], p)) for i, p in enumerate(row_peers)]
    def ring(buf, index, up, down, send, recv):
        here, above, below = index(0), index(1), index(3)
        first = [
            go(remote(buf.at[here], buf.at[here], send.at[0], recv.at[0], up)),
            go(remote(buf.at[here], buf.at[here], send.at[1], recv.at[1], down)),
        ]

        def second():
            low, high = pl.ds(0, 8), pl.ds(8, 8)
            out = []
            first[0].wait_recv()
            out.append(go(remote(buf.at[below, :, low], buf.at[below, :, low], send.at[2], recv.at[2], up)))
            first[1].wait_recv()
            out.append(go(remote(buf.at[above, :, high], buf.at[above, :, high], send.at[3], recv.at[3], down)))
            return out

        return second

    def x_index(i, side):
        return (yhi if side == 0 else 1 - yhi) * 8 + lax.rem(x + i, 4) * 2 + core

    def x_ring(side):
        return ring(cent_i, lambda i: x_index(i, side), x_up, x_down, xsend.at[side], xrecv.at[side])

    relays = []

    def to_core(side, i):
        part = cent_i.at[x_index(i, side)]
        relays.append(go(remote(part, part, xsend.at[side, 4 + i], xrecv.at[side, 4 + i], core_peer)))

    yi_copy = go(remote(cent_i.at[c], cent_i.at[c], ysend.at[0], yrecv.at[0], y_far))
    x_second = x_ring(0)
    z_second = ring(cent_j, lambda i: zs[i], z_up, z_down, zsend, zrecv)
    to_core(0, 0)

    lane = lax.broadcasted_iota(jnp.int32, (BLK, 128), 1) % 4
    ri = lax.broadcasted_iota(jnp.int32, (128, 128), 0)
    ci = lax.broadcasted_iota(jnp.int32, (128, 128), 1)

    def spread(turned_rows, chosen):
        k = lax.broadcasted_iota(jnp.int32, (turned_rows.shape[1], 128), 0)
        return jnp.dot(turned_rows, jnp.where(chosen(k), 1.0, 0.0).astype(BF16), preferred_element_type=F32)

    def apply(halves, column, dj):
        part = None
        to_cols = []
        for q in range(4):
            blk = halves[q // 2][:, (q % 2) * 128 : (q % 2) * 128 + 128]
            e = blk * dj[:, q * 128 : (q + 1) * 128]
            part = e if part is None else part + e
            to_cols.append(jnp.sum(blk * column, axis=0, keepdims=True))
        to_rows = jnp.sum(jnp.transpose(part), axis=0, keepdims=True)
        return to_rows, jnp.concatenate(to_cols, axis=1)

    def masks(a, b, s, count):
        used = row_mask(s, count, lambda m, n: m < n)
        other = row_mask((b ^ (r * BPD + within(a))) | (owner_of(a) ^ c), 0, lambda m, n: m != n)
        return used, used & other

    def near_left(s, _):
        k = within(stage[s])
        p = blocks[k]
        mid = [jnp.mean(p[d]) for d in range(3)]
        put_rows(abuf, left_rows(*(p[d] - mid[d] for d in range(3)), p[3]))
        put_rows(abuf.at[120:123], split3(own_dens[pl.ds(k, 1), :]))
        at = jnp.transpose(abuf[...]).astype(BF16)
        for u in range(4):
            lhs[s, u] = jnp.where(lane == u, at, jnp.zeros_like(at))
        turned[s] = spread(at, lambda k: (k >= 120) & (k < 123))
        for d in range(3):
            mids[s, d : d + 1, :] = jnp.full((1, BLK), mid[d], F32)
        return 0

    def near_right(s, p, dj):
        put_rows(bbuf, right_rows(*(p[d] - mids[s, d : d + 1, :] for d in range(3)), p[3]))
        bt = bbuf[...].astype(BF16)
        rhs[0] = bt
        for t in range(1, 4):
            shift = jnp.where((ri // 4 == ci // 4) & ((ri % 4 + t) % 4 == ci % 4), 1.0, 0.0).astype(BF16)
            rhs[t] = jnp.dot(shift, bt, preferred_element_type=F32).astype(BF16)
        for h in range(2):
            span = slice(h * 256, (h + 1) * 256)
            for i in range(2):
                rows = slice(i * 256, (i + 1) * 256)
                acc = None
                for t in range(4):
                    for u in range(4):
                        v = lax.rsqrt(jnp.dot(lhs[s, u, rows, :], rhs[t][:, span], preferred_element_type=F32))
                        acc = v if acc is None else acc + v
                tile[rows, span] = acc
        to_rows, to_cols = apply([tile.at[:, 0:256], tile.at[:, 256:512]], turned[s], dj)
        used, mirror = masks(stage[s], stage[NNEAR + s], s, ncount[0])
        near_all[8, pl.ds(s, 1), :] = jnp.where(used, to_rows, 0.0)
        near_all[7, pl.ds(s, 1), :] = jnp.where(mirror, to_cols, 0.0)

    def wanted(row, s):
        return lists[row, NNEAR + 1 + s]

    def item_mask(a, b):
        return jnp.full((4, 4, BLK), a, jnp.int32) == jnp.full((4, 4, BLK), b, jnp.int32)

    def a_copy(way, s):
        return remote(apack.at[s, way], agot.at[s, way], asend.at[way, s], arecv.at[way, s], (z_up, z_down)[way])

    def b_copy(way, s):
        return remote(bpack.at[s, way], bgot.at[s, way], bsend.at[way, s], brecv.at[way, s], (z_up, z_down)[way])

    def n_copy(s):
        return remote(cpack.at[s], cgot.at[s], nsend.at[s], nrecv.at[s], y_near)

    def step_a(s, _):
        for way in range(2):
            apack[s, way] = blocks[within(wanted(zs[2] * 2 + way, s))]
            a_copy(way, s).start()
        return 0

    def step_b(s, _):
        for way in range(2):
            to = zs[1 if way == 0 else 3] * 2
            bpack[s, way, 1 - way] = blocks[within(wanted(to + 1 - way, s))]
            b = wanted(to + way, s)
            a_copy(way, s).wait_recv()
            bpack[s, way, way] = jnp.where(item_mask(owner_of(b), r), blocks[within(b)], agot[s, way])
            b_copy(way, s).start()
        return 0

    def assembled(y, s):
        b = wanted(z * 2 + y, s)
        oz = lax.shift_right_logical(owner_of(b), 1)
        above = (oz ^ zs[1]) * ((oz ^ zs[2]) | (y ^ 1))
        v = jnp.where(item_mask(above, 0), bgot[s, 1, y], bgot[s, 0, y])
        return jnp.where(item_mask(oz, z), blocks[within(b)], v)

    def step_c(s, _):
        for way in range(2):
            b_copy(way, s).wait_recv()
        cpack[s] = assembled(1 - ylo, s)
        n_copy(s).start()
        return 0

    def near_slot(s):
        n_copy(s).wait_recv()
        b = stage[NNEAR + 1 + s]
        owner = owner_of(b)
        pj[...] = jnp.where(item_mask(owner & 1, ylo), assembled(ylo, s), cgot[s])
        here = cent_j[lax.shift_right_logical(owner, 1), 4, pl.ds(within(b), 1), :]
        d = jnp.where(same_rows(owner & 1, ylo), here, got_d[pl.ds(s, 1), :])
        near_right(s + 1, pj, d)

    for m in range(7, 9):
        near_all[m] = jnp.zeros((8, BLK), F32)
    lax.fori_loop(0, 2, near_left, 0)

    for copy in list_copies:
        copy.wait_recv()
    lax.fori_loop(0, NREM, step_a, 0)
    x_half = x_second()
    z_half = z_second()
    to_core(0, 3)
    to_core(0, 1)

    k0 = within(stage[0])
    pj[...] = blocks[k0]
    near_right(0, pj, own_dens[pl.ds(k0, 1), :])

    lax.fori_loop(0, NREM, step_b, 0)
    yi_copy.wait_recv()
    x_second = x_ring(1)
    to_core(1, 0)
    lax.fori_loop(2, NNEAR, near_left, 0)
    for copy in x_half:
        copy.wait_recv()
    to_core(0, 2)

    for copy in z_half:
        copy.wait_recv()
    near_row = y_near[0]
    for s in range(NREM):
        b = wanted(near_row, s)
        sel_d[s : s + 1, :] = cent_j[lax.shift_right_logical(owner_of(b), 1), 4, pl.ds(within(b), 1), :]
    yd_copy = go(remote(sel_d, got_d, ysend.at[2], yrecv.at[2], y_near))

    def choose_j(s, _):
        b = lists[near_row, 32 + s]
        g, k = lax.shift_right_logical(owner_of(b), 1), within(b)
        for f in range(5):
            sel_j[f, pl.ds(s, 1), :] = cent_j[g, f, pl.ds(k, 1), :]
        return 0

    lax.fori_loop(0, NFAR, choose_j, 0)
    yj_copy = go(remote(sel_j, got_j, ysend.at[1], yrecv.at[1], y_near))
    lax.fori_loop(0, 2, step_c, 0)
    x_half = x_second()
    to_core(1, 3)
    to_core(1, 1)
    yd_copy.wait_recv()
    near_slot(0)
    for copy in x_half:
        copy.wait_recv()
    to_core(1, 2)
    lax.fori_loop(2, NREM, step_c, 0)
    near_slot(1)

    yj_copy.wait_recv()
    for copy in relays:
        copy.wait_recv()

    def take(s, _):
        a, b = stage[16 + s], stage[32 + s]
        one = pl.ds(s, 1)
        for f in range(5):
            far_i[f, one, :] = cent_i[owner_of(a), f, pl.ds(within(a), 1), :]
        owner, k = owner_of(b), within(b)
        here = same_rows(owner & 1, ylo)
        for f in range(5):
            far_j[f, one, :] = jnp.where(
                here, cent_j[lax.shift_right_logical(owner, 1), f, pl.ds(k, 1), :], got_j[f, one, :]
            )
        return 0

    lax.fori_loop(0, NFAR, take, 0)
    for d in range(3):
        mid = jnp.mean(far_i[d], axis=1, keepdims=True)
        far_i[d] = far_i[d] - mid
        far_j[d] = far_j[d] - mid

    at_lane = lax.broadcasted_iota(jnp.int32, (1, BLK), 1)

    def ids_of(values, n):
        ids = jnp.full((1, BLK), -1, jnp.int32)
        for s in range(n):
            ids = jnp.where(at_lane == s, values(s), ids)
        return ids.astype(F32)

    for ref, first in ((rows_all.at[0], 16), (cols_far, 32)):
        ref[16:, :] = jnp.zeros((8, BLK), F32)
        ref[16:17, :] = ids_of(lambda s, first=first: stage[first + s], NFAR)

    for g in range(2):
        eight = slice(g * 8, g * 8 + 8)
        put_rows(fa, left_rows(*(far_i[d, eight, :] for d in range(4))))
        put_rows(fb, right_rows(*(far_j[d, eight, :] for d in range(4))))
        put_rows(fd, split3(far_i[4, eight, :]))
        fat[g] = jnp.transpose(fa[...]).astype(BF16)
        fbt[g] = fb[...].astype(BF16)
        fdt[g] = jnp.transpose(fd[...]).astype(BF16)
    far_lane = lax.broadcasted_iota(jnp.int32, (BLK, 256), 1) % 8

    def far(i, _):
        for n in range(2):
            s = 2 * i + n
            g, e = s // 8, lax.rem(s, 8)
            one = pl.ds(s, 1)
            at = fat[g]
            at = jnp.where(far_lane == e, at, jnp.zeros_like(at))
            halves = [
                lax.rsqrt(jnp.dot(at, fbt[g, :, h * 256 : (h + 1) * 256], preferred_element_type=F32))
                for h in range(2)
            ]
            column = spread(fdt[g], lambda k, e=e: (k % 8 == e) & (k < 24))
            to_rows, to_cols = apply(halves, column, far_j[4, one, :])
            used, mirror = masks(stage[16 + s], stage[32 + s], s, fcount[0])
            rows_all[0, one, :] = jnp.where(used, to_rows, 0.0)
            cols_far[one, :] = jnp.where(mirror, to_cols, 0.0)
        return 0

    lax.fori_loop(0, NFAR // 2, far, 0)
    m_copy = go(remote(rows_all.at[0], rows_all.at[1], msend.at[0], mrecv.at[0], y_far))
    lax.fori_loop(2, 4, lambda s, v: (near_slot(s), v)[1], 0)

    m_copy.wait_recv()
    total = gathered(rows_all, yhi * 128, 128, 16)
    for g in range(8):
        half[g] = total[g * BPD : (g + 1) * BPD, :]
    p_copies = []
    for i, p in enumerate(xc_peers):
        to = lax.rem(xc + 1 + i, 8)
        p_copies.append(go(remote(half.at[to], parts.at[i], psend.at[i], precv.at[i], p)))

    total = scatter(cols_far[16:17, 0:24].astype(jnp.int32), 0, 128, cols_far[...])
    for g in range(8):
        side[g] = total[g * BPD : (g + 1) * BPD, :]
    f_copies = [
        go(remote(side.at[lax.rem(r + 1 + i, N_ROW)], side_got.at[i], fsend.at[i], frecv.at[i], p))
        for i, p in enumerate(row_peers)
    ]

    near_slot(4)

    near_all[8, 6:7, :] = ids_of(lambda s: within(stage[s]) + r * BPD, NNEAR)
    near_all[7, 6:7, :] = ids_of(lambda s: stage[NNEAR + s], NNEAR)
    c_copies = [
        go(remote(near_all.at[7], near_all.at[i], csend.at[i], crecv.at[i], p)) for i, p in enumerate(row_peers)
    ]
    acc = half[xc] + side[r]
    for i, copy in enumerate(f_copies):
        copy.wait_recv()
        acc = acc + side_got[i]
    for i, copy in enumerate(p_copies):
        copy.wait_recv()
        acc = acc + parts[i]
    for copy in c_copies:
        copy.wait_recv()
    acc = acc + gathered(near_all, r * BPD, BPD, 6)
    for q in range(4):
        out[pl.ds(q, BPD, stride=4), :] = acc[:, q * 128 : (q + 1) * 128]
    for copy in started:
        copy.wait_send()

    def sent(s, _):
        for way in range(2):
            a_copy(way, s).wait_send()
            b_copy(way, s).wait_send()
        n_copy(s).wait_send()
        return 0

    lax.fori_loop(0, NREM, sent, 0)


def body(points, density, near_pairs, far_pairs, near_count, far_count):
    dma = pltpu.SemaphoreType.DMA
    smem = pl.BlockSpec(memory_space=pltpu.SMEM)
    hbm = pl.BlockSpec(memory_space=pltpu.HBM)
    out = pl.pallas_call(
        potential_kernel,
        out_shape=jax.ShapeDtypeStruct((BPD * 4, 128), F32),
        in_specs=[hbm, hbm, smem, smem, hbm, hbm],
        out_specs=pl.BlockSpec(memory_space=pltpu.VMEM),
        scratch_shapes=[
            pltpu.SMEM((1,), jnp.int32),
            pltpu.SMEM((1,), jnp.int32),
            pltpu.SMEM((N_ROW, LIST), jnp.int32),
            pltpu.SMEM((LIST,), jnp.int32),
            vmem(BPD, 4, 4, BLK),
            vmem(BPD * 4, 128),
            vmem(N_COL, 5, BPD, BLK),
            vmem(4, 5, BPD, BLK),
            vmem(BPD, BLK),
            vmem(5, NFAR, BLK),
            vmem(5, NFAR, BLK),
            vmem(8, BLK),
            vmem(8, BLK),
            vmem(5, NFAR, BLK),
            vmem(5, NFAR, BLK),
            vmem(NREM, 2, 4, 4, BLK),
            vmem(NREM, 2, 4, 4, BLK),
            vmem(NREM, 2, 2, 4, 4, BLK),
            vmem(NREM, 2, 2, 4, 4, BLK),
            vmem(NREM, 4, 4, BLK),
            vmem(NREM, 4, 4, BLK),
            vmem(128, BLK),
            vmem(128, BLK),
            vmem(NNEAR, BLK, 128),
            vmem(NNEAR, 8, BLK),
            vmem(NNEAR, 4, BLK, 128, dtype=BF16),
            vmem(4, 128, BLK, dtype=BF16),
            vmem(BLK, BLK),
            vmem(4, 4, BLK),
            vmem(256, BLK),
            vmem(256, BLK),
            vmem(32, BLK),
            vmem(2, BLK, 256, dtype=BF16),
            vmem(2, 256, BLK, dtype=BF16),
            vmem(2, BLK, 32, dtype=BF16),
            vmem(2, 24, BLK),
            vmem(24, BLK),
            vmem(9, 8, BLK),
            vmem(8, BPD, BLK),
            vmem(7, BPD, BLK),
            vmem(8, BPD, BLK),
            vmem(7, BPD, BLK),
            dma((BPD + 3,)),
            dma((7,)), dma((7,)), dma((2, 8)), dma((2, 8)), dma((4,)), dma((4,)),
            dma((2, NREM)), dma((2, NREM)), dma((2, NREM)), dma((2, NREM)), dma((NREM,)), dma((NREM,)), dma((3,)), dma((3,)),
            dma((1,)), dma((1,)), dma((7,)), dma((7,)), dma((7,)), dma((7,)), dma((7,)), dma((7,)),
        ],
        compiler_params=pltpu.CompilerParams(collective_id=0, has_side_effects=True, vmem_limit_bytes=64 << 20),
    )(points, density.reshape(-1, 128), near_pairs.T, far_pairs.T, near_count, far_count)
    return out.reshape(-1)


def solution(mesh):
    in_specs = (
        P(None, None, ("row", "col")),
        P(("row", "col")),
        P(("row", "col"), None),
        P(("row", "col"), None),
        P(("row", "col")),
        P(("row", "col")),
    )
    out_specs = P(("row", "col"))
    return jax.shard_map(body, mesh=mesh, in_specs=in_specs, out_specs=out_specs, check_vma=False)
```
